32 devices in a mesh: pix: 8 (over z, x), ang: 4 (over y, core).
Axes of the slice: x: 2, y: 2, z: 4, core: 2. Of those that a mesh axis runs over, the one named last changes fastest.
Arguments:
- volume: float32 [256, 128, 128], P(('pix', 'ang')), may hold values from -6 to 6
- projector: float32 [5120, 128, 128], P(('pix', 'ang')), may hold values from -0.078125 to 0.078125
- tile_ids: int32 [5120], P(('pix', 'ang')), may hold values from 0 to 1023, as said below
- counts: int32 [128, 128, 128], P('ang'), may hold values from 64 to 4095
- ray_counts: int32 [4, 8], P('ang'), may hold values from 1 to 4, 20 in all within a row
Outputs:
- updated: float32 [256, 128, 128], P(('pix', 'ang'))
The draws below stay inside these ranges and needn't reach their ends.
Inputs may be any that keep to these rules, and one draw needn't show every extreme that they name: `tile_ids`: within each device's aligned block of 160 entries the values are distinct; value v names ray block v // 32 and pixel tile v % 32 of that device. `ray_counts`: each row sums to 20; the largest entry of every row is 4.
All inputs are finite; a program needn't handle non-finite values.
Results may differ from the reference program's by a relative error of at most 0.0001.
Values sent between devices are 32-bit elements; how exact they have to be, the bound alone decides.
No kernel may reach another device: no remote copies, remote signals or barrier semaphores. Data moves between devices by JAX's collectives and lax.ppermute only.
A program may use at most 128 MiB of HBM per device.

```python
import math
import jax
import jax.numpy as jnp
import numpy as np
from jax import lax

TILE = 128
SL = 128
PT = 32
MOST = 4
K = 160
RB = 32
LIVE = 20
TILES_ALL = 5120
VOXEL_TILES = 256
RAY_ROWS = 128
N_PIX = 8
N_ANG = 4


def draw_tile_ids(key, part):
    device_keys = jax.random.split(key, N_PIX * N_ANG)
    chosen = jax.vmap(lambda device_key: jax.random.permutation(device_key, RB * PT)[:K])(device_keys)
    return chosen.reshape(-1).astype(jnp.int32)


def place_ends(array, own_key, smallest, largest):
    longest = array.shape.index(max(array.shape))
    spots = []
    for shift in (0, 1):
        where = [jax.random.randint(jax.random.fold_in(own_key, axis), (), 0, length) for axis, length in enumerate(array.shape)]
        where[longest] = (where[longest] + shift) % array.shape[longest]
        spots.append(tuple(where))
    return array.at[spots[0]].set(smallest).at[spots[1]].set(largest)


def shard_levels(key, shape, pieces, smallest, high):
    factor_of = 1.0
    for dim, parts in pieces:
        heights = jax.random.uniform(jax.random.fold_in(jax.random.fold_in(key, 6), dim), (parts,), jnp.float32, smallest / len(pieces), high / len(pieces))
        factor_of = factor_of * jnp.repeat(jnp.exp(heights), shape[dim] // parts).reshape((-1,) + (1,) * (len(shape) - 1 - dim))
    return factor_of


def length_profile(number_of, total, most, skew):
    portions = [(1 << 20) // math.isqrt(standing ** skew) + 1 for standing in range(2, number_of + 1)]
    rest, holding = total - most - (number_of - 1), [1] * (number_of - 1)
    while rest > 0:
        free = [i for i in range(number_of - 1) if holding[i] < most]
        mass, remaining = sum([portions[i] for i in free]), rest
        for i in free:
            more = min(most - holding[i], max(1, remaining * portions[i] // mass), rest)
            holding[i] = holding[i] + more
            rest = rest - more
    return np.array([most] + holding)


def ragged_sizes(own_key, number_of, total, bound, skew):
    if number_of == 2:
        one = jax.random.randint(own_key, (), max(1, total - bound), min(bound, total - 1) + 1)
        return jnp.stack([one, total - one])
    tallies = jnp.asarray(length_profile(number_of, total, bound, skew), jnp.int32)
    pairs = (number_of - 1) // 2
    source_of, receiver = tallies[1:1 + 2 * pairs:2], tallies[2:2 + 2 * pairs:2]
    slack = jnp.minimum(source_of - 1, bound - receiver)
    shifted = jax.random.randint(jax.random.fold_in(own_key, 1), (pairs,), 0, 1 << 20) % (slack + 1)
    tallies = tallies.at[1:1 + 2 * pairs:2].set(source_of - shifted).at[2:2 + 2 * pairs:2].set(receiver + shifted)
    return tallies[jax.random.permutation(jax.random.fold_in(own_key, 2), number_of)]


def centred(rng, dims, spread, bound, cuts=(), kind=jnp.bfloat16):
    result = spread * jax.random.normal(rng, dims, jnp.float32)
    if cuts:
        result = result * shard_levels(rng, dims, cuts, -0.22, 0.18)
    return jnp.clip(result, -bound, bound).astype(kind)


def setup_inputs(seed: int = 0) -> dict:
    seeds = jax.random.split(jax.random.key(seed), 6)
    volume = centred(seeds[0], (VOXEL_TILES, SL, TILE), 1.0, 6.0, ((0, 32),), jnp.float32)
    projector = centred(seeds[1], (TILES_ALL, TILE, TILE), (TILE * K // MOST) ** -0.5, 0.078125, ((0, 32),), jnp.float32)
    tile_ids = draw_tile_ids(jax.random.fold_in(seeds[5], 71), 0)
    counts = place_ends(jax.random.randint(seeds[3], (RAY_ROWS, SL, TILE), 64, 4096), jax.random.fold_in(seeds[3], 1), 64, 4095).astype(jnp.int32)
    ray_counts = jax.vmap(lambda own: ragged_sizes(own, N_PIX, LIVE, MOST, 2))(jax.random.split(seeds[4], N_ANG)).reshape((N_ANG, N_PIX)).astype(jnp.int32)
    return dict(volume=volume, projector=projector, tile_ids=tile_ids, counts=counts, ray_counts=ray_counts)


blank_flux = 4096.0
step_size = 0.5


def reference(volume, projector, tile_ids, counts, ray_counts):
    highest = lax.Precision.HIGHEST
    device_total = N_PIX * N_ANG
    device_ids = jnp.arange(device_total, dtype=jnp.int32)
    pix_owner = device_ids // N_ANG
    angle_group = device_ids % N_ANG
    local_ids = tile_ids.reshape(device_total, K)
    ray_rows = (angle_group[:, None] * RB + local_ids // PT).astype(jnp.int32)
    pixel_cols = (pix_owner[:, None] * PT + local_ids % PT).astype(jnp.int32)
    blocks_all = projector.reshape(device_total, K, TILE, TILE)

    def forward(running, inputs):
        blocks, row_index, col_index = inputs
        picked = jnp.take(volume, col_index, axis=0)
        product = jnp.einsum("ksq,krq->ksr", picked, blocks, precision=highest)
        return running.at[row_index].add(product), None

    projected = lax.scan(forward, jnp.zeros((N_ANG * RB, SL, TILE), jnp.float32), (blocks_all, ray_rows, pixel_cols))[0]
    slot_index = jnp.arange(RB, dtype=jnp.int32)
    live_mask = (slot_index % MOST)[None, :] < ray_counts[:, slot_index // MOST]
    live_mask = live_mask.reshape(N_ANG * RB)[:, None, None]
    measured = counts.astype(jnp.float32)
    weights = jnp.where(live_mask, measured / blank_flux, 0.0)
    measured_data = jnp.where(live_mask, jnp.log(blank_flux / measured), 0.0)
    residual = weights * (projected - measured_data)

    def backward(running, inputs):
        blocks, row_index, col_index = inputs
        picked = jnp.take(residual, row_index, axis=0)
        product = jnp.einsum("ksr,krq->ksq", picked, blocks, precision=highest)
        return running.at[col_index].add(product), None

    gradient = lax.scan(backward, jnp.zeros((N_PIX * PT, SL, TILE), jnp.float32), (blocks_all, ray_rows, pixel_cols))[0]
    return volume - step_size * gradient
```

```python
import functools

import jax
import jax.numpy as jnp
from jax import lax
from jax.experimental import pallas as pl
from jax.experimental.pallas import tpu as pltpu
from jax.sharding import PartitionSpec as P

blank_flux = 4096.0
step_size = 0.5
unroll = 8
chunk = 16
vmem_bytes = 40 * 1024 * 1024

smem = pl.BlockSpec(memory_space=pltpu.SMEM)
vmem = pl.BlockSpec(memory_space=pltpu.VMEM)
anywhere = pl.BlockSpec(memory_space=pl.ANY)
params = pltpu.CompilerParams(vmem_limit_bytes=vmem_bytes)
f32, bf16, i32 = jnp.float32, jnp.bfloat16, jnp.int32


def halves(value):
    high = value.astype(bf16)
    return high, (value - high.astype(f32)).astype(bf16)


def plan_kernel(own_tiles, pixel_tiles, live_total, ids, rays, place, counts, rank_of, col_of, tile_of, total, picked, slot_rank, sem):
    tile_count = ids.shape[0]
    ray_blocks = counts.shape[0]
    capacity = ray_blocks // rays.shape[1]
    piece = picked.shape[1]
    start = pl.multiple_of(place[0], piece)

    def slot(j, rank):
        live = lax.rem(j, capacity) < rays[0, lax.div(j, capacity)]
        slot_rank[j] = jnp.where(live, rank, -1)

        @pl.when(live)
        def _():
            pltpu.make_async_copy(counts.at[j, pl.ds(start, piece)], picked.at[rank], sem).start()

        return rank + live.astype(i32)

    lax.fori_loop(0, ray_blocks, slot, jnp.int32(0))

    def tile(t, n):
        value = ids[t]
        rank = slot_rank[lax.div(value, pixel_tiles)]
        col = lax.rem(value, pixel_tiles)
        owner = lax.div(col, own_tiles)
        rank_of[n] = rank
        col_of[n] = (owner ^ place[1]) * own_tiles + lax.rem(col, own_tiles)
        tile_of[n] = t
        return n + (rank >= 0).astype(i32)

    n = lax.fori_loop(0, tile_count, tile, jnp.int32(0))
    for extra in range(unroll):
        rank_of[n + extra] = live_total
        col_of[n + extra] = pixel_tiles
        tile_of[n + extra] = 0
    total[0] = n
    pltpu.make_async_copy(picked, picked, sem).wait()


def split_kernel(projector, out):
    step = min(chunk, projector.shape[0])
    width = projector.shape[2]

    def body(index, block):
        high, low = halves(block[...])
        rows = pl.ds(index[0] * step, step)
        out[rows, :, :width] = high
        out[rows, :, width:] = low

    pltpu.emit_pipeline(
        lambda block: body((pl.program_id(0),), block),
        grid=(projector.shape[0] // step,),
        in_specs=[pl.BlockSpec((step,) + projector.shape[1:], lambda i: (i, 0, 0))],
    )(projector)


def forward_kernel(angles, deep, rank_of, col_of, tile_of, total, place, split, *refs):
    tiles, outs, (packed, sums) = refs[:angles], refs[angles : angles + deep], refs[angles + deep :]
    own_tiles, half, width = tiles[0].shape
    piece = half // deep

    for a in range(angles):

        def fill(i, carry, a=a):
            for k in range(deep):
                rows = pl.ds(pl.multiple_of((place[2] ^ k) * piece, piece), piece)
                high, low = halves(tiles[a][i, rows, :])
                for side in range(2):
                    lanes = slice(side * width, (side + 1) * width)
                    packed[a * own_tiles + i, k * piece : (k + 1) * piece, lanes] = high
                    packed[a * own_tiles + i, half + k * piece : half + (k + 1) * piece, lanes] = low
            return carry

        lax.fori_loop(0, own_tiles, fill, 0)
    sums[...] = jnp.zeros_like(sums)

    def step(i, carry):
        products = []
        for u in range(unroll):
            j = i * unroll + u
            product = lax.dot_general(
                packed[col_of[j]], split[tile_of[j]], (((1,), (1,)), ((), ())), preferred_element_type=f32
            )
            products.append(product[:half] + product[half:])
        for u in range(unroll):
            sums[rank_of[i * unroll + u]] += products[u]
        return carry

    lax.fori_loop(0, lax.div(total[0] + unroll - 1, unroll), step, 0)
    for k in range(deep):
        out = outs[k]
        out[...] = sums[: out.shape[0], k * piece : (k + 1) * piece, :]


def backward_kernel(angles, deep, rank_of, col_of, tile_of, total, split, *refs):
    blocks, outs, (packed, sums) = refs[:deep], refs[deep : deep + angles], refs[deep + angles :]
    live, piece, width = blocks[0].shape
    half = piece * deep
    own_tiles = outs[0].shape[0]
    for k in range(deep):

        def fill(i, carry, k=k):
            high, low = halves(blocks[k][i])
            packed[i, k * piece : (k + 1) * piece, :] = high
            packed[i, half + k * piece : half + (k + 1) * piece, :] = low
            return carry

        lax.fori_loop(0, live, fill, 0)
    sums[...] = jnp.zeros_like(sums)

    def step(i, carry):
        products = []
        for u in range(unroll):
            j = i * unroll + u
            product = jnp.dot(packed[rank_of[j]], split[tile_of[j]], preferred_element_type=f32)
            product = product[:half] + product[half:]
            products.append(product[:, :width] + product[:, width:])
        for u in range(unroll):
            sums[col_of[i * unroll + u]] += products[u]
        return carry

    lax.fori_loop(0, lax.div(total[0] + unroll - 1, unroll), step, 0)
    for a in range(angles):
        outs[a][...] = sums[a * own_tiles : (a + 1) * own_tiles]


def add_kernel(left, right, out):
    out[...] = left[...] + right[...]


def residual_kernel(counts, *refs):
    *terms, out = refs
    summed = terms[0][...]
    for term in terms[1:]:
        summed = summed + term[...]
    measured = counts[...].astype(f32)
    out[...] = measured / blank_flux * (summed - jnp.log(blank_flux / measured))


def update_kernel(deep, place, volume, *refs):
    *terms, out = refs
    half = terms[0].shape[1]
    piece = half // deep
    per_half = len(terms) // 2
    for side in range(2):
        base = (place[3] ^ side) * half
        for k in range(deep):
            rows = pl.ds(pl.multiple_of(base + (place[2] ^ k) * piece, piece), piece)
            local = slice(k * piece, (k + 1) * piece)
            gradient = terms[side * per_half][:, local, :]
            for term in terms[side * per_half + 1 : (side + 1) * per_half]:
                gradient = gradient + term[:, local, :]
            out[:, rows, :] = volume[:, rows, :] - step_size * gradient


def call(kernel, out_shape, in_specs, scratch=(), out_specs=None):
    if out_specs is None:
        out_specs = jax.tree.map(lambda leaf: vmem, out_shape)
    return pl.pallas_call(
        kernel,
        out_shape=out_shape,
        in_specs=in_specs,
        out_specs=out_specs,
        scratch_shapes=list(scratch),
        compiler_params=params,
    )


def add(left, right):
    return call(add_kernel, jax.ShapeDtypeStruct(left.shape, f32), [vmem, vmem])(left, right)


def shards(volume, projector, tile_ids, counts, ray_counts):
    pix, ang = lax.axis_size("pix"), lax.axis_size("ang")
    own_tiles, slices, width = volume.shape
    ray_blocks = counts.shape[0]
    tile_count, rays, _ = projector.shape
    pixel_tiles = own_tiles * ang
    live = ray_blocks * 5 // 8
    deep = pix // 2
    half, piece = slices // 2, slices // pix
    me, angle = lax.axis_index("pix"), lax.axis_index("ang")
    side, depth = me % 2, me // 2
    place = jnp.stack([side * half + depth * piece, angle, depth, side]).astype(i32)

    across = lambda value, axis, flip: lax.ppermute(
        value, axis, [(d, d ^ flip) for d in range(lax.axis_size(axis))]
    )
    angle_bits = [1 << b for b in range(ang.bit_length() - 1)]

    def spread(value):
        held = {0: value}
        for bit in reversed(angle_bits):
            held.update({k ^ bit: across(part, "ang", bit) for k, part in list(held.items())})
        return [held[k] for k in range(ang)]

    far = lax.dynamic_slice_in_dim(volume, (1 - side) * half, half, 1)
    near = lax.dynamic_slice_in_dim(volume, side * half, half, 1)
    far_tiles = spread(far)
    near_tiles = spread(near)

    listed = jax.ShapeDtypeStruct((tile_count + unroll,), i32)
    rank_of, col_of, tile_of, total, picked = call(
        functools.partial(plan_kernel, own_tiles, pixel_tiles, live),
        (listed, listed, listed, jax.ShapeDtypeStruct((1,), i32), jax.ShapeDtypeStruct((live, piece, rays), i32)),
        [smem, smem, smem, anywhere],
        [pltpu.SMEM((ray_blocks,), i32), pltpu.SemaphoreType.DMA],
        (smem, smem, smem, smem, vmem),
    )(tile_ids, ray_counts, place, counts)
    lists = (rank_of, col_of, tile_of, total)

    split = call(split_kernel, pltpu.VMEM((tile_count, rays, 2 * width), bf16), [anywhere], (), vmem)(projector)

    def forward(tiles):
        return call(
            functools.partial(forward_kernel, ang, deep),
            (jax.ShapeDtypeStruct((live, piece, rays), f32),) * deep,
            [smem] * 5 + [vmem] * (1 + ang),
            [
                pltpu.VMEM((pixel_tiles + 1, 2 * half, 2 * width), bf16),
                pltpu.VMEM((live + 1, half, rays), f32),
            ],
        )(*lists, place, split, *tiles)

    def backward(blocks):
        return call(
            functools.partial(backward_kernel, ang, deep),
            (jax.ShapeDtypeStruct((own_tiles, half, width), f32),) * ang,
            [smem] * 4 + [vmem] * (1 + deep),
            [
                pltpu.VMEM((live + 1, 2 * half, rays), bf16),
                pltpu.VMEM((pixel_tiles + 1, half, width), f32),
            ],
        )(*lists, split, *blocks)

    far_parts = forward(far_tiles)
    order = list(range(deep - 1, -1, -1))
    crossed = {k: across(far_parts[k], "pix", 1) for k in order}
    near_parts = forward(near_tiles)
    arrived = [across(add(near_parts[k], crossed[k]), "pix", 2 * k) for k in order if k]
    own = call(
        residual_kernel, jax.ShapeDtypeStruct((live, piece, rays), f32), [vmem] * (3 + len(arrived))
    )(picked, near_parts[0], crossed[0], *arrived)

    near_blocks = [own] + [across(own, "pix", 2 * k) for k in range(1, deep)]
    far_blocks = [across(block, "pix", 1) for block in near_blocks]

    def gather(parts):
        parts = dict(enumerate(parts))
        for bit in angle_bits[:-1]:
            for k in [k for k in parts if k & bit]:
                moved = across(parts.pop(k), "ang", bit)
                parts[k ^ bit] = add(parts[k ^ bit], moved)
        last = angle_bits[-1]
        return [parts[0], across(parts[last], "ang", last)]

    terms = gather(backward(near_blocks)) + gather(backward(far_blocks))
    return call(
        functools.partial(update_kernel, deep), jax.ShapeDtypeStruct(volume.shape, f32), [smem] + [vmem] * 5
    )(place, volume, *terms)


def solution(mesh):
    placed = (
        P(("pix", "ang"), None, None),
        P(("pix", "ang"), None, None),
        P(("pix", "ang")),
        P("ang", None, None),
        P("ang", None),
    )
    return jax.shard_map(
        shards, mesh=mesh, in_specs=placed, out_specs=P(("pix", "ang"), None, None), check_vma=False
    )
```

```python
import functools

import jax
import jax.numpy as jnp
from jax import lax
from jax.experimental import pallas as pl
from jax.experimental.pallas import tpu as pltpu
from jax.sharding import PartitionSpec as P

blank_flux = 4096.0
step_size = 0.5
unroll = 8
group = 8
vmem_bytes = 40 * 1024 * 1024

smem = pl.BlockSpec(memory_space=pltpu.SMEM)
vmem = pl.BlockSpec(memory_space=pltpu.VMEM)
hbm = pl.BlockSpec(memory_space=pltpu.HBM)
params = pltpu.CompilerParams(vmem_limit_bytes=vmem_bytes)
f32, bf16, i32 = jnp.float32, jnp.bfloat16, jnp.int32


def halves(value):
    high = value.astype(bf16)
    return high, (value - high.astype(f32)).astype(bf16)


def front_kernel(own_tiles, angles, live_total, ids_hbm, rays_hbm, place, counts, projector, rank_of, col_of, tile_of, total, picked, split, ids, rays, slot_rank, block, fetched, sem, sides):
    copies = [
        pltpu.make_async_copy(ids_hbm, ids, sides.at[0]),
        pltpu.make_async_copy(rays_hbm, rays, sides.at[1]),
    ]
    for copy in copies:
        copy.start()
    for copy in copies:
        copy.wait()
    tile_count = ids.shape[0]
    span = tile_count + unroll
    pixel_tiles = own_tiles * angles
    ray_blocks = counts.shape[0]
    capacity = ray_blocks // rays.shape[1]
    piece = picked.shape[1]
    width = block.shape[2]
    start = pl.multiple_of(place[0], piece)
    for a in range(angles):
        total[a] = 0

    def slot(j, rank):
        live = lax.rem(j, capacity) < rays[0, lax.div(j, capacity)]
        slot_rank[j] = jnp.where(live, rank, -1)

        @pl.when(live)
        def _():
            pltpu.make_async_copy(counts.at[j, pl.ds(start, piece)], picked.at[rank], sem).start()

        return rank + live.astype(i32)

    lax.fori_loop(0, ray_blocks, slot, jnp.int32(0), unroll=4)

    def fetch(t, n):
        pltpu.make_async_copy(projector.at[t], block.at[n], fetched.at[lax.div(n, group)]).start()

    def tile(t, n):
        value = ids[t]
        rank = slot_rank[lax.div(value, pixel_tiles)]

        @pl.when(rank >= 0)
        def _():
            fetch(t, n)
            col = lax.rem(value, pixel_tiles)
            turn = lax.div(col, own_tiles) ^ place[1]
            at = total[turn]
            total[turn] = at + 1
            at = turn * span + at
            rank_of[at] = rank
            col_of[at] = turn * own_tiles + lax.rem(col, own_tiles)
            tile_of[at] = n

        return n + (rank >= 0).astype(i32)

    n = lax.fori_loop(0, tile_count, tile, jnp.int32(0), unroll=4)
    groups = lax.div(n + group - 1, group)

    def fill(extra, carry):
        fetch(0, extra)
        return carry

    lax.fori_loop(n, groups * group, fill, 0)
    for a in range(angles):
        for extra in range(unroll):
            at = a * span + total[a] + extra
            rank_of[at] = live_total
            col_of[at] = pixel_tiles
            tile_of[at] = 0

    def halve(g, carry):
        rows = pl.ds(g * group, group)
        pltpu.make_async_copy(block.at[rows], block.at[rows], fetched.at[g]).wait()
        for u in range(group):
            high, low = halves(block[g * group + u])
            split[g * group + u, :, :width] = high
            split[g * group + u, :, width:] = low
        return carry

    lax.fori_loop(0, groups, halve, 0)
    pltpu.make_async_copy(picked, picked, sem).wait()


def each(turns, span, total, product, sums, index):
    for a in turns:

        def step(i, carry, a=a):
            base = a * span + i * unroll
            products = [product(base + u) for u in range(unroll)]
            for u in range(unroll):
                sums[index[base + u]] += products[u]
            return carry

        lax.fori_loop(0, lax.div(total[a] + unroll - 1, unroll), step, 0)


def forward_kernel(turns, span, deep, chained, rank_of, col_of, tile_of, total, place, split, *refs):
    tiles, refs = refs[: len(turns)], refs[len(turns) :]
    before, refs = refs[:chained], refs[chained:]
    *outs, packed, sums = refs
    own_tiles, half, width = tiles[0].shape
    piece = half // deep

    for a, tile in zip(turns, tiles):

        def fill(i, carry, a=a, tile=tile):
            for k in range(deep):
                rows = pl.ds(pl.multiple_of((place[2] ^ k) * piece, piece), piece)
                high, low = halves(tile[i, rows, :])
                for side in range(2):
                    lanes = slice(side * width, (side + 1) * width)
                    packed[a * own_tiles + i, k * piece : (k + 1) * piece, lanes] = high
                    packed[a * own_tiles + i, half + k * piece : half + (k + 1) * piece, lanes] = low
            return carry

        lax.fori_loop(0, own_tiles, fill, 0)
    sums[...] = before[0][...] if chained else jnp.zeros_like(sums)

    def product(j):
        both = lax.dot_general(
            packed[col_of[j]], split[tile_of[j]], (((1,), (1,)), ((), ())), preferred_element_type=f32
        )
        return both[:half] + both[half:]

    each(turns, span, total, product, sums, rank_of)
    if len(outs) == 1:
        outs[0][...] = sums[...]
        return
    for k in range(deep):
        out = outs[k]
        out[...] = sums[: out.shape[0], k * piece : (k + 1) * piece, :]


def backward_kernel(turns, span, deep, rank_of, col_of, tile_of, total, split, *refs):
    blocks, refs = refs[:deep], refs[deep:]
    *outs, packed, sums = refs
    live, piece, width = blocks[0].shape
    half = piece * deep
    own_tiles = outs[0].shape[0]
    for k in range(deep):

        def fill(i, carry, k=k):
            high, low = halves(blocks[k][i])
            packed[i, k * piece : (k + 1) * piece, :] = high
            packed[i, half + k * piece : half + (k + 1) * piece, :] = low
            return carry

        lax.fori_loop(0, live, fill, 0, unroll=4)
    for a in turns:
        sums[a * own_tiles : (a + 1) * own_tiles] = jnp.zeros_like(outs[0])

    def product(j):
        both = jnp.dot(packed[rank_of[j]], split[tile_of[j]], preferred_element_type=f32)
        both = both[:half] + both[half:]
        return both[:, :width] + both[:, width:]

    each(turns, span, total, product, sums, col_of)
    for a, out in zip(turns, outs):
        out[...] = sums[a * own_tiles : (a + 1) * own_tiles]


def add_kernel(left, right, out):
    out[...] = left[...] + right[...]


def residual_kernel(counts, *refs):
    *terms, out = refs
    summed = terms[0][...]
    for term in terms[1:]:
        summed = summed + term[...]
    measured = counts[...].astype(f32)
    out[...] = measured / blank_flux * (summed - jnp.log(blank_flux / measured))


def update_kernel(deep, place, volume, *refs):
    *terms, out = refs
    half = terms[0].shape[1]
    piece = half // deep
    per_half = len(terms) // 2
    for side in range(2):
        base = (place[3] ^ side) * half
        for k in range(deep):
            rows = pl.ds(pl.multiple_of(base + (place[2] ^ k) * piece, piece), piece)
            local = slice(k * piece, (k + 1) * piece)
            gradient = terms[side * per_half][:, local, :]
            for term in terms[side * per_half + 1 : (side + 1) * per_half]:
                gradient = gradient + term[:, local, :]
            out[:, rows, :] = volume[:, rows, :] - step_size * gradient


def call(kernel, out_shape, in_specs, scratch=(), out_specs=None, traffic=None):
    if out_specs is None:
        out_specs = jax.tree.map(lambda leaf: vmem, out_shape)
    return pl.pallas_call(
        kernel,
        out_shape=out_shape,
        in_specs=in_specs,
        out_specs=out_specs,
        scratch_shapes=list(scratch),
        compiler_params=params,
        cost_estimate=None if traffic is None else pl.CostEstimate(flops=0, bytes_accessed=traffic, transcendentals=0),
    )


def in_hbm(value):
    return pltpu.with_memory_space_constraint(value, pltpu.HBM)


def add(left, right):
    return call(add_kernel, jax.ShapeDtypeStruct(left.shape, f32), [vmem, vmem])(left, right)


def shards(volume, projector, tile_ids, counts, ray_counts):
    pix, ang = lax.axis_size("pix"), lax.axis_size("ang")
    own_tiles, slices, width = volume.shape
    ray_blocks = counts.shape[0]
    tile_count, rays, _ = projector.shape
    pixel_tiles = own_tiles * ang
    live = ray_blocks * 5 // 8
    deep = pix // 2
    half, piece = slices // 2, slices // pix
    me, angle = lax.axis_index("pix"), lax.axis_index("ang")
    side, depth = me % 2, me // 2
    place = jnp.stack([side * half + depth * piece, angle, depth, side]).astype(i32)

    across = lambda value, axis, flip: lax.ppermute(
        value, axis, [(d, d ^ flip) for d in range(lax.axis_size(axis))]
    )
    angle_bits = [1 << b for b in range(ang.bit_length() - 1)]

    def after(value, *others):
        return lax.optimization_barrier((value,) + others)[0]

    def spread(value):
        top = angle_bits[-1]
        return {0: value, top: across(value, "ang", top), 1: across(value, "ang", 1)}

    def relay(held, *others):
        top = angle_bits[-1]
        held = dict(held)
        held[top ^ 1] = across(after(held[top], *others), "ang", 1)
        for bit in angle_bits[1:-1]:
            held.update({k ^ bit: across(part, "ang", bit) for k, part in list(held.items())})
        return held

    far = lax.dynamic_slice_in_dim(volume, (1 - side) * half, half, 1)
    near = lax.dynamic_slice_in_dim(volume, side * half, half, 1)
    far_tiles = spread(far)
    near_tiles = spread(near)

    span = tile_count + unroll
    stored = -(-tile_count // group) * group
    heavy = projector.size * 4
    listed = jax.ShapeDtypeStruct((ang * span,), i32)
    rank_of, col_of, tile_of, total, picked, split = call(
        functools.partial(front_kernel, own_tiles, ang, live),
        (
            listed,
            listed,
            listed,
            jax.ShapeDtypeStruct((ang,), i32),
            jax.ShapeDtypeStruct((live, piece, rays), i32),
            pltpu.VMEM((stored, rays, 2 * width), bf16),
        ),
        [hbm, hbm, smem, hbm, hbm],
        [
            pltpu.SMEM(tile_ids.shape, i32),
            pltpu.SMEM(ray_counts.shape, i32),
            pltpu.SMEM((ray_blocks,), i32),
            pltpu.VMEM((stored, rays, width), f32),
            pltpu.SemaphoreType.DMA((stored // group,)),
            pltpu.SemaphoreType.DMA,
            pltpu.SemaphoreType.DMA((2,)),
        ],
        (smem, smem, smem, smem, vmem, vmem),
        None,
    )(in_hbm(tile_ids), in_hbm(ray_counts), place, in_hbm(counts), in_hbm(projector))
    lists = (rank_of, col_of, tile_of)
    rows = jax.ShapeDtypeStruct((live, piece, rays), f32)
    columns = jax.ShapeDtypeStruct((own_tiles, half, width), f32)

    def forward(turns, tiles, before=(), final=True):
        return call(
            functools.partial(forward_kernel, turns, span, deep, len(before)),
            (rows,) * deep if final else pltpu.VMEM((live + 1, half, rays), f32),
            [smem] * 5 + [vmem] * (1 + len(turns) + len(before)),
            [
                pltpu.VMEM((pixel_tiles + 1, 2 * half, 2 * width), bf16),
                pltpu.VMEM((live + 1, half, rays), f32),
            ],
            traffic=None,
        )(*lists, total, place, split, *[tiles[a] for a in turns], *before)

    def backward(turns, blocks, total):
        parts = call(
            functools.partial(backward_kernel, turns, span, deep),
            (columns,) * len(turns),
            [smem] * 4 + [vmem] * (1 + deep),
            [
                pltpu.VMEM((live + 1, 2 * half, rays), bf16),
                pltpu.VMEM((pixel_tiles + 1, half, width), f32),
            ],
            traffic=None,
        )(*lists, total, split, *blocks)
        return dict(zip(turns, parts))

    turns = tuple(range(ang))
    early = tuple(k for k in turns if k < 2)
    late = turns[2:]
    far_sums = forward(early, far_tiles, (), False)
    near_sums = forward(early, near_tiles, (), False)
    far_tiles = relay(far_tiles, far_sums)
    near_tiles = relay(near_tiles, near_sums)
    far_parts = forward(late, far_tiles, (after(far_sums, near_sums),))
    order = list(range(deep - 1, -1, -1))
    crossed = {k: across(far_parts[k], "pix", 1) for k in order}
    near_parts = forward(late, near_tiles, (near_sums,))
    arrived = [across(add(near_parts[k], crossed[k]), "pix", 2 * k) for k in order if k]
    own = call(
        residual_kernel, jax.ShapeDtypeStruct((live, piece, rays), f32), [vmem] * (3 + len(arrived))
    )(picked, near_parts[0], crossed[0], *arrived)

    near_blocks = [own] + [across(own, "pix", 2 * k) for k in range(1, deep)]
    far_blocks = [across(block, "pix", 1) for block in near_blocks]

    def gather(blocks, total, cuts, *others):
        odd, parts = {}, {}
        for at, cut in enumerate(cuts):
            if at:
                total = after(total, *others)
            made = backward(cut, blocks, total)
            odd.update({k ^ 1: across(part, "ang", 1) for k, part in made.items() if k & 1})
            parts.update({k: part for k, part in made.items() if not k & 1})
        parts = {k: part + odd[k] for k, part in parts.items()}
        for bit in angle_bits[1:-1]:
            for k in [k for k in parts if k & bit]:
                moved = across(parts.pop(k), "ang", bit)
                parts[k ^ bit] = parts[k ^ bit] + moved
        last = parts[angle_bits[-1]]
        return [parts[0], across(last, "ang", angle_bits[-1])], last

    terms, sent = gather(near_blocks, total, (turns,))
    terms = terms + gather(far_blocks, total, (turns[1::2], turns[::2]), sent)[0]
    return call(
        functools.partial(update_kernel, deep), jax.ShapeDtypeStruct(volume.shape, f32), [smem] + [vmem] * 5
    )(place, volume, *terms)


def solution(mesh):
    placed = (
        P(("pix", "ang"), None, None),
        P(("pix", "ang"), None, None),
        P(("pix", "ang")),
        P("ang", None, None),
        P("ang", None),
    )
    return jax.shard_map(
        shards, mesh=mesh, in_specs=placed, out_specs=P(("pix", "ang"), None, None), check_vma=False
    )
```

```python
import functools

import jax
import jax.numpy as jnp
from jax import lax
from jax.experimental import pallas as pl
from jax.experimental.pallas import tpu as pltpu
from jax.sharding import PartitionSpec as P

blank_flux = 4096.0
step_size = 0.5
unroll = 8
group = 8
vmem_bytes = 40 * 1024 * 1024

smem = pl.BlockSpec(memory_space=pltpu.SMEM)
vmem = pl.BlockSpec(memory_space=pltpu.VMEM)
hbm = pl.BlockSpec(memory_space=pltpu.HBM)
anywhere = pl.BlockSpec(memory_space=pl.ANY)
params = pltpu.CompilerParams(vmem_limit_bytes=vmem_bytes)
f32, bf16, i32 = jnp.float32, jnp.bfloat16, jnp.int32


def halves(value):
    high = value.astype(bf16)
    return high, (value - high.astype(f32)).astype(bf16)


def front_kernel(own_tiles, angles, live_total, ids_hbm, rays_hbm, place, counts, projector, rank_of, col_of, tile_of, total, picked, split, ids, rays, slot_rank, block, fetched, sem, sides):
    copies = [
        pltpu.make_async_copy(ids_hbm, ids, sides.at[0]),
        pltpu.make_async_copy(rays_hbm, rays, sides.at[1]),
    ]
    for copy in copies:
        copy.start()
    for copy in copies:
        copy.wait()
    tile_count = ids.shape[0]
    span = tile_count + unroll
    pixel_tiles = own_tiles * angles
    ray_blocks = counts.shape[0]
    capacity = ray_blocks // rays.shape[1]
    piece = picked.shape[1]
    width = block.shape[2]
    start = pl.multiple_of(place[0], piece)
    for a in range(angles):
        total[a] = 0

    def slot(j, rank):
        live = lax.rem(j, capacity) < rays[0, lax.div(j, capacity)]
        slot_rank[j] = jnp.where(live, rank, -1)

        @pl.when(live)
        def _():
            pltpu.make_async_copy(counts.at[j, pl.ds(start, piece)], picked.at[rank], sem).start()

        return rank + live.astype(i32)

    lax.fori_loop(0, ray_blocks, slot, jnp.int32(0), unroll=4)

    def fetch(t, n):
        pltpu.make_async_copy(projector.at[t], block.at[n], fetched.at[lax.div(n, group)]).start()

    def tile(t, n):
        value = ids[t]
        rank = slot_rank[lax.div(value, pixel_tiles)]

        @pl.when(rank >= 0)
        def _():
            fetch(t, n)
            col = lax.rem(value, pixel_tiles)
            turn = lax.div(col, own_tiles) ^ place[1]
            at = total[turn]
            total[turn] = at + 1
            at = turn * span + at
            rank_of[at] = rank
            col_of[at] = turn * own_tiles + lax.rem(col, own_tiles)
            tile_of[at] = n

        return n + (rank >= 0).astype(i32)

    n = lax.fori_loop(0, tile_count, tile, jnp.int32(0), unroll=4)
    groups = lax.div(n + group - 1, group)

    def fill(extra, carry):
        fetch(0, extra)
        return carry

    lax.fori_loop(n, groups * group, fill, 0)
    for a in range(angles):
        for extra in range(unroll):
            at = a * span + total[a] + extra
            rank_of[at] = live_total
            col_of[at] = pixel_tiles
            tile_of[at] = 0

    def halve(g, carry):
        rows = pl.ds(g * group, group)
        pltpu.make_async_copy(block.at[rows], block.at[rows], fetched.at[g]).wait()
        for u in range(group):
            high, low = halves(block[g * group + u])
            split[g * group + u, :, :width] = high
            split[g * group + u, :, width:] = low
        return carry

    lax.fori_loop(0, groups, halve, 0)
    pltpu.make_async_copy(picked, picked, sem).wait()


def each(turns, span, total, product, sums, index):
    for a in turns:

        def step(i, carry, a=a):
            base = a * span + i * unroll
            products = [product(base + u) for u in range(unroll)]
            for u in range(unroll):
                sums[index[base + u]] += products[u]
            return carry

        lax.fori_loop(0, lax.div(total[a] + unroll - 1, unroll), step, 0)


def forward_kernel(turns, sides, span, deep, chained, rank_of, col_of, tile_of, total, place, split, *refs):
    tiles, refs = refs[: sides * len(turns)], refs[sides * len(turns) :]
    before, refs = refs[:chained], refs[chained:]
    *outs, packed, sums = refs
    own_tiles, half, width = tiles[0].shape
    piece = half // deep
    rows_all = sides * half

    for at, a in enumerate(turns):

        def fill(i, carry, at=at, a=a):
            for part in range(sides):
                for k in range(deep):
                    rows = pl.ds(pl.multiple_of((place[2] ^ k) * piece, piece), piece)
                    first = part * half + k * piece
                    high, low = halves(tiles[part * len(turns) + at][i, rows, :])
                    for side in range(2):
                        lanes = slice(side * width, (side + 1) * width)
                        packed[a * own_tiles + i, first : first + piece, lanes] = high
                        packed[a * own_tiles + i, rows_all + first : rows_all + first + piece, lanes] = low
            return carry

        lax.fori_loop(0, own_tiles, fill, 0)
    sums[...] = before[0][...] if chained else jnp.zeros_like(sums)

    def product(j):
        both = lax.dot_general(
            packed[col_of[j]], split[tile_of[j]], (((1,), (1,)), ((), ())), preferred_element_type=f32
        )
        return both[:rows_all] + both[rows_all:]

    each(turns, span, total, product, sums, rank_of)
    if not chained:
        for part, out in enumerate(outs):
            out[...] = sums[:, part * half : (part + 1) * half, :]
        return
    for k, out in enumerate(outs):
        out[...] = sums[: out.shape[0], k * piece : (k + 1) * piece, :]


def backward_kernel(turns, loose, layout, span, rank_of, col_of, tile_of, total, split, *refs):
    *refs, packed, sums = refs
    refs = list(refs)
    blocks = [[refs.pop(0) for _ in range(parts)] for parts in layout]
    outs, count = refs, len(layout)
    live, _, width = blocks[0][0].shape
    rows_all = packed.shape[1] // 2
    piece = rows_all // count
    own_tiles = outs[0].shape[0]
    zeros = jnp.zeros((own_tiles, rows_all, width), f32)
    for k, block in enumerate(blocks):

        def fill(i, carry, k=k, block=block):
            whole = jnp.concatenate([part[i] for part in block], axis=0)
            high, low = halves(whole)
            packed[i, k * piece : (k + 1) * piece, :] = high
            packed[i, rows_all + k * piece : rows_all + (k + 1) * piece, :] = low
            return carry

        lax.fori_loop(0, live, fill, 0, unroll=4)
    for a in turns:
        sums[a * own_tiles : (a + 1) * own_tiles] = zeros

    def product(j):
        both = jnp.dot(packed[rank_of[j]], split[tile_of[j]], preferred_element_type=f32)
        both = both[:rows_all] + both[rows_all:]
        return both[:, :width] + both[:, width:]

    each(turns, span, total, product, sums, col_of)
    for a in turns:
        tiles = slice(a * own_tiles, (a + 1) * own_tiles)
        if a not in loose:
            outs.pop(0)[...] = sums[tiles]
            continue
        for k in range(count):
            outs.pop(0)[...] = sums[tiles, k * piece : (k + 1) * piece, :]


def add_kernel(cuts, count, *refs):
    terms, outs = refs[:count], refs[count:]
    for first, out in zip(cuts, outs):
        rows = out.shape[1]
        total = None
        for term in terms:
            value = term[...] if term.shape[1] == rows else term[:, first : first + rows, :]
            total = value if total is None else total + value
        out[...] = total


def residual_kernel(cuts, counts, *refs):
    terms, outs = refs[: -len(cuts)], refs[-len(cuts) :]
    height = counts.shape[1]
    summed = 0.0
    parts = [term[...] for term in terms if term.shape[1] == height]
    for part in parts:
        summed = summed + part
    short = [term[...] for term in terms if term.shape[1] != height]
    if short:
        upper = sum(short[:-1])
        summed = summed + jnp.concatenate([upper, short[-1]], axis=1)
    measured = counts[...].astype(f32)
    value = measured / blank_flux * (summed - jnp.log(blank_flux / measured))
    for first, out in zip(cuts, outs):
        out[...] = value[:, first : first + out.shape[1], :]


def update_kernel(parts, deep, place, volume, *refs):
    terms, (out, fresh, sems) = refs[: 2 * len(parts)], refs[-3:]
    half = fresh.shape[1] // 2
    piece = half // deep
    copies = []
    for at, part in enumerate(parts):
        left, right = terms[2 * at : 2 * at + 2]
        for slot, (flip, k) in enumerate(part):
            first = (place[3] ^ flip) * half + (place[2] ^ k) * piece
            rows = pl.ds(pl.multiple_of(first, piece), piece)
            local = slice(slot * piece, (slot + 1) * piece)
            fresh[:, rows, :] = volume[:, rows, :] - step_size * (left[:, local, :] + right[:, local, :])
            copies.append(pltpu.make_async_copy(fresh.at[:, rows], out.at[:, rows], sems.at[len(copies)]))
            copies[-1].start()
    for copy in copies:
        copy.wait()


def call(kernel, out_shape, in_specs, scratch=(), out_specs=None, traffic=None):
    if out_specs is None:
        out_specs = jax.tree.map(lambda leaf: vmem, out_shape)
    return pl.pallas_call(
        kernel,
        out_shape=out_shape,
        in_specs=in_specs,
        out_specs=out_specs,
        scratch_shapes=list(scratch),
        compiler_params=params,
        cost_estimate=None if traffic is None else pl.CostEstimate(flops=0, bytes_accessed=traffic, transcendentals=0),
    )


def in_hbm(value):
    return pltpu.with_memory_space_constraint(value, pltpu.HBM)


def add(cuts, rows, *terms):
    live, _, width = terms[0].shape
    return call(
        functools.partial(add_kernel, cuts, len(terms)),
        (jax.ShapeDtypeStruct((live, rows, width), f32),) * len(cuts),
        [vmem] * len(terms),
    )(*terms)


def shards(volume, projector, tile_ids, counts, ray_counts):
    pix, ang = lax.axis_size("pix"), lax.axis_size("ang")
    own_tiles, slices, width = volume.shape
    ray_blocks = counts.shape[0]
    tile_count, rays, _ = projector.shape
    pixel_tiles = own_tiles * ang
    live = ray_blocks * 5 // 8
    deep = pix // 2
    half, piece = slices // 2, slices // pix
    me, angle = lax.axis_index("pix"), lax.axis_index("ang")
    side, depth = me % 2, me // 2
    place = jnp.stack([side * half + depth * piece, angle, depth, side]).astype(i32)

    across = lambda value, axis, flip: lax.ppermute(
        value, axis, [(d, d ^ flip) for d in range(lax.axis_size(axis))]
    )
    angle_bits = [1 << b for b in range(ang.bit_length() - 1)]

    def after(value, *others):
        return lax.optimization_barrier((value,) + others)[0]

    def spread(value):
        top = angle_bits[-1]
        return {0: value, top: across(value, "ang", top), 1: across(value, "ang", 1)}

    def relay(held, *others):
        top = angle_bits[-1]
        held = dict(held)
        held[top ^ 1] = across(after(held[top], *others), "ang", 1)
        for bit in angle_bits[1:-1]:
            held.update({k ^ bit: across(part, "ang", bit) for k, part in list(held.items())})
        return held

    far = lax.dynamic_slice_in_dim(volume, (1 - side) * half, half, 1)
    near = lax.dynamic_slice_in_dim(volume, side * half, half, 1)
    far_tiles = spread(far)
    near_tiles = spread(near)

    span = tile_count + unroll
    stored = -(-tile_count // group) * group
    heavy = projector.size * 4
    listed = jax.ShapeDtypeStruct((ang * span,), i32)
    rank_of, col_of, tile_of, total, picked, split = call(
        functools.partial(front_kernel, own_tiles, ang, live),
        (
            listed,
            listed,
            listed,
            jax.ShapeDtypeStruct((ang,), i32),
            jax.ShapeDtypeStruct((live, piece, rays), i32),
            pltpu.VMEM((stored, rays, 2 * width), bf16),
        ),
        [hbm, hbm, smem, hbm, hbm],
        [
            pltpu.SMEM(tile_ids.shape, i32),
            pltpu.SMEM(ray_counts.shape, i32),
            pltpu.SMEM((ray_blocks,), i32),
            pltpu.VMEM((stored, rays, width), f32),
            pltpu.SemaphoreType.DMA((stored // group,)),
            pltpu.SemaphoreType.DMA,
            pltpu.SemaphoreType.DMA((2,)),
        ],
        (smem, smem, smem, smem, vmem, vmem),
        None,
    )(in_hbm(tile_ids), in_hbm(ray_counts), place, in_hbm(counts), in_hbm(projector))
    lists = (rank_of, col_of, tile_of)
    rows = jax.ShapeDtypeStruct((live, piece, rays), f32)
    columns = jax.ShapeDtypeStruct((own_tiles, half, width), f32)

    def forward(turns, sides, before=()):
        count = len(sides)
        return call(
            functools.partial(forward_kernel, turns, count, span, deep, len(before)),
            (rows,) * deep if before else (pltpu.VMEM((live + 1, half, rays), f32),) * count,
            [smem] * 5 + [vmem] * (1 + count * len(turns) + len(before)),
            [
                pltpu.VMEM((pixel_tiles + 1, 2 * count * half, 2 * width), bf16),
                pltpu.VMEM((live + 1, count * half, rays), f32),
            ],
        )(*lists, total, place, split, *[tiles[a] for tiles in sides for a in turns], *before)

    def backward(turns, part, total, loose=()):
        count = len(part)
        height = piece * count
        made = call(
            functools.partial(backward_kernel, turns, loose, [len(blocks[spot]) for spot in part], span),
            sum(
                (
                    (jax.ShapeDtypeStruct((own_tiles, piece, width), f32),) * count
                    if a in loose
                    else (jax.ShapeDtypeStruct((own_tiles, height, width), f32),)
                    for a in turns
                ),
                (),
            ),
            [smem] * 4 + [vmem] * (1 + sum(len(blocks[spot]) for spot in part)),
            [
                pltpu.VMEM((live + 1, 2 * height, rays), bf16),
                pltpu.VMEM((pixel_tiles + 1, height, width), f32),
            ],
        )(*lists, total, split, *[block for spot in part for block in blocks[spot]])
        made = list(made)
        return {a: [made.pop(0) for _ in range(count if a in loose else 1)] for a in turns}

    turns = tuple(range(ang))
    early = tuple(k for k in turns if k < 2)
    late = turns[2:]
    far_sums, near_sums = forward(early, (far_tiles, near_tiles))
    far_tiles = relay(far_tiles, total)
    near_tiles = relay(near_tiles, near_sums)
    far_parts = forward(late, (far_tiles,), (far_sums,))
    order = [k for k in (3, 2, 1) if k < deep] + list(range(4, deep)) + [0]
    crossed = {k: across(far_parts[k], "pix", 1) for k in order}
    near_parts = forward(late, (near_tiles,), (near_sums,))
    def residual(cuts, heights, *terms):
        return call(
            functools.partial(residual_kernel, cuts),
            tuple(jax.ShapeDtypeStruct((live, height, rays), f32) for height in heights),
            [vmem] * (1 + len(terms)),
        )(picked, *terms)

    side_of = lambda value, k: across(value, "pix", 2 * k)
    cut = piece // 2
    if deep == 4:
        first, rest = add((0, cut), cut, near_parts[3], crossed[3])
        came = [side_of(first, 3)]
        passed = side_of(rest, 1)
        (first,) = add((0,), cut, near_parts[2], crossed[2])
        came.append(side_of(first, 2))
        (rest,) = add((cut,), cut, near_parts[2], crossed[2], after(passed, came[0]))
        rest = side_of(rest, 2)
        (one,) = add((0,), piece, after(near_parts[1], first), crossed[1])
        whole_one = side_of(one, 1)
        own, first, last = residual(
            (0, 0, cut), (piece, cut, cut), near_parts[0], crossed[0], *came, rest, whole_one
        )
        last_two = side_of(last, 2)
        near_one = side_of(own, 1)
        first_three = side_of(first, 3)
        first_two = side_of(first, 2)
        last_three = side_of(last_two, 1)
        near_blocks = [(own,), (near_one,), (first_two, last_two), (first_three, last_three)]
    else:
        came = [side_of(add((0,), piece, near_parts[k], crossed[k])[0], k) for k in order if k]
        (own,) = residual((0,), (piece,), near_parts[0], crossed[0], *came)
        near_blocks = [(own,)] + [(side_of(own, k),) for k in range(1, deep)]
    far_blocks = [tuple(across(part, "pix", 1) for part in parts) for parts in near_blocks]
    blocks = {(0, k): parts for k, parts in enumerate(near_blocks)}
    blocks.update({(1, k): parts for k, parts in enumerate(far_blocks)})
    arrival = [k for k in (1, 3, 2) if k < deep] + list(range(4, deep))
    near_all = [(0, k) for k in [0] + arrival]
    far_all = [(1, k) for k in [0] + arrival]
    top = angle_bits[-1]
    lower, upper = turns[:top], turns[top:]

    def join(parts):
        return jnp.concatenate(parts, axis=1) if len(parts) > 1 else parts[0]

    def fold(parts, *others):
        parts = dict(parts)
        for bit in angle_bits[:-1]:
            for k in [k for k in parts if k & bit]:
                moved = [across(after(part, *others), "ang", bit) for part in parts.pop(k)]
                parts[k ^ bit] = [join(parts[k ^ bit]) + join(moved)]
        return parts[min(parts)][0]

    def whole(part, total, *others):
        made = backward(turns, part, total, upper[1::2])
        return fold({k: made[k] for k in lower}, *others), fold({k: made[k] for k in upper}, *others)

    def update(parts, terms, *started):
        return pl.pallas_call(
            functools.partial(update_kernel, parts, deep),
            out_shape=jax.ShapeDtypeStruct(volume.shape, f32),
            in_specs=[smem] + [vmem] * (1 + len(terms)) + [anywhere] * len(started),
            out_specs=anywhere,
            scratch_shapes=[pltpu.VMEM(volume.shape, f32), pltpu.SemaphoreType.DMA((2 * deep,))],
            input_output_aliases={2 + len(terms): 0} if started else {},
            compiler_params=params,
        )(place, volume, *terms, *started)

    made = backward(turns, near_all, total)
    up_near = fold({k: made[k] for k in upper})
    low_near = fold({k: made[k] for k in lower})
    up_far = fold(backward(upper, far_all, total))
    low_far = fold(backward(lower, far_all, after(total, up_near, up_far)))
    came_near = across(up_near, "ang", top)
    came_far = across(up_far, "ang", top)
    begun = update((near_all,), (low_near, came_near))
    return update((far_all,), (low_far, came_far), begun)


def solution(mesh):
    placed = (
        P(("pix", "ang"), None, None),
        P(("pix", "ang"), None, None),
        P(("pix", "ang")),
        P("ang", None, None),
        P("ang", None),
    )
    return jax.shard_map(
        shards, mesh=mesh, in_specs=placed, out_specs=P(("pix", "ang"), None, None), check_vma=False
    )
```

```python
import functools

import jax
import jax.numpy as jnp
from jax import lax
from jax.experimental import pallas as pl
from jax.experimental.pallas import tpu as pltpu
from jax.sharding import PartitionSpec as P

blank_flux = 4096.0
step_size = 0.5
unroll = 20
group = 8
vmem_bytes = 40 * 1024 * 1024

smem = pl.BlockSpec(memory_space=pltpu.SMEM)
vmem = pl.BlockSpec(memory_space=pltpu.VMEM)
hbm = pl.BlockSpec(memory_space=pltpu.HBM)
anywhere = pl.BlockSpec(memory_space=pl.ANY)
params = pltpu.CompilerParams(vmem_limit_bytes=vmem_bytes)
f32, bf16, i32 = jnp.float32, jnp.bfloat16, jnp.int32


def halves(value):
    high = value.astype(bf16)
    return high, (value - high.astype(f32)).astype(bf16)


def front_kernel(own_tiles, angles, live_total, ids_hbm, rays_hbm, place, counts, projector, rank_of, col_of, tile_of, total, picked, split, ids, rays, slot_rank, block, fetched, sem, sides):
    copies = [
        pltpu.make_async_copy(ids_hbm, ids, sides.at[0]),
        pltpu.make_async_copy(rays_hbm, rays, sides.at[1]),
    ]
    for copy in copies:
        copy.start()
    for copy in copies:
        copy.wait()
    tile_count = ids.shape[0]
    span = tile_count + unroll
    pixel_tiles = own_tiles * angles
    ray_blocks = counts.shape[0]
    capacity = ray_blocks // rays.shape[1]
    piece = picked.shape[1]
    width = block.shape[2]
    start = pl.multiple_of(place[0], piece)
    for a in range(2):
        total[a] = 0

    def slot(j, rank):
        live = lax.rem(j, capacity) < rays[0, lax.div(j, capacity)]
        slot_rank[j] = jnp.where(live, rank, -1)

        @pl.when(live)
        def _():
            pltpu.make_async_copy(counts.at[j, pl.ds(start, piece)], picked.at[rank], sem).start()

        return rank + live.astype(i32)

    lax.fori_loop(0, ray_blocks, slot, jnp.int32(0), unroll=4)

    def fetch(t, n):
        pltpu.make_async_copy(projector.at[t], block.at[n], fetched.at[lax.div(n, group)]).start()

    def tile(t, n):
        value = ids[t]
        rank = slot_rank[lax.div(value, pixel_tiles)]

        @pl.when(rank >= 0)
        def _():
            fetch(t, n)
            col = lax.rem(value, pixel_tiles)
            turn = lax.div(col, own_tiles) ^ place[1]
            group_of = lax.div(turn, angles // 2)
            at = total[group_of]
            total[group_of] = at + 1
            at = group_of * span + at
            rank_of[at] = rank
            col_of[at] = turn * own_tiles + lax.rem(col, own_tiles)
            tile_of[at] = n

        return n + (rank >= 0).astype(i32)

    n = lax.fori_loop(0, tile_count, tile, jnp.int32(0), unroll=4)
    groups = lax.div(n + group - 1, group)

    def fill(extra, carry):
        fetch(0, extra)
        return carry

    lax.fori_loop(n, groups * group, fill, 0)
    for a in range(2):
        for extra in range(unroll):
            at = a * span + total[a] + extra
            rank_of[at] = live_total
            col_of[at] = pixel_tiles
            tile_of[at] = 0

    def halve(g, carry):
        rows = pl.ds(g * group, group)
        pltpu.make_async_copy(block.at[rows], block.at[rows], fetched.at[g]).wait()
        for u in range(group):
            high, low = halves(block[g * group + u])
            split[g * group + u, :, :width] = high
            split[g * group + u, :, width:] = low
        return carry

    lax.fori_loop(0, groups, halve, 0)
    pltpu.make_async_copy(picked, picked, sem).wait()


def each(lists, span, total, product, sums, index):
    for a in lists:

        def step(i, carry, a=a):
            base = a * span + i * unroll
            products = [product(base + u) for u in range(unroll)]
            for u in range(unroll):
                sums[index[base + u]] += products[u]
            return carry

        lax.fori_loop(0, lax.div(total[a] + unroll - 1, unroll), step, 0)


def forward_kernel(turns, lists, sides, span, deep, chained, rank_of, col_of, tile_of, total, place, split, *refs):
    tiles, refs = refs[: sides * len(turns)], refs[sides * len(turns) :]
    before, refs = refs[:chained], refs[chained:]
    *outs, packed, sums = refs
    own_tiles, half, width = tiles[0].shape
    piece = half // deep
    rows_all = sides * half

    for at, a in enumerate(turns):

        def fill(i, carry, at=at, a=a):
            for part in range(sides):
                for k in range(deep):
                    rows = pl.ds(pl.multiple_of((place[2] ^ k) * piece, piece), piece)
                    first = part * half + k * piece
                    high, low = halves(tiles[part * len(turns) + at][i, rows, :])
                    for side in range(2):
                        lanes = slice(side * width, (side + 1) * width)
                        packed[a * own_tiles + i, first : first + piece, lanes] = high
                        packed[a * own_tiles + i, rows_all + first : rows_all + first + piece, lanes] = low
            return carry

        lax.fori_loop(0, own_tiles, fill, 0)
    sums[...] = before[0][...] if chained else jnp.zeros_like(sums)

    def product(j):
        both = lax.dot_general(
            packed[col_of[j]], split[tile_of[j]], (((1,), (1,)), ((), ())), preferred_element_type=f32
        )
        return both[:rows_all] + both[rows_all:]

    each(lists, span, total, product, sums, rank_of)
    if not chained:
        for part, out in enumerate(outs):
            out[...] = sums[:, part * half : (part + 1) * half, :]
        return
    for k, out in enumerate(outs):
        out[...] = sums[: out.shape[0], k * piece : (k + 1) * piece, :]


def backward_kernel(turns, lists, loose, count, span, rank_of, col_of, tile_of, total, split, *refs):
    *refs, packed, sums = refs
    blocks, outs = refs[:count], list(refs[count:])
    live, piece, width = blocks[0].shape
    rows_all = piece * count
    own_tiles = outs[0].shape[0]
    zeros = jnp.zeros((own_tiles, rows_all, width), f32)
    for k, block in enumerate(blocks):

        def fill(i, carry, k=k, block=block):
            high, low = halves(block[i])
            packed[i, k * piece : (k + 1) * piece, :] = high
            packed[i, rows_all + k * piece : rows_all + (k + 1) * piece, :] = low
            return carry

        lax.fori_loop(0, live, fill, 0, unroll=4)
    for a in turns:
        sums[a * own_tiles : (a + 1) * own_tiles] = zeros

    def product(j):
        both = jnp.dot(packed[rank_of[j]], split[tile_of[j]], preferred_element_type=f32)
        both = both[:rows_all] + both[rows_all:]
        return both[:, :width] + both[:, width:]

    each(lists, span, total, product, sums, col_of)
    for a in turns:
        tiles = slice(a * own_tiles, (a + 1) * own_tiles)
        if a not in loose:
            outs.pop(0)[...] = sums[tiles]
            continue
        for k in range(count):
            outs.pop(0)[...] = sums[tiles, k * piece : (k + 1) * piece, :]


def add_kernel(left, right, out):
    out[...] = left[...] + right[...]


def residual_kernel(counts, *refs):
    *terms, out = refs
    summed = terms[0][...]
    for term in terms[1:]:
        summed = summed + term[...]
    measured = counts[...].astype(f32)
    out[...] = measured / blank_flux * (summed - jnp.log(blank_flux / measured))


def update_kernel(parts, deep, place, volume, *refs):
    terms, (out, fresh, sems) = refs[: 2 * len(parts)], refs[-3:]
    half = fresh.shape[1] // 2
    piece = half // deep
    copies = []
    for at, part in enumerate(parts):
        left, right = terms[2 * at : 2 * at + 2]
        for slot, (flip, k) in enumerate(part):
            first = (place[3] ^ flip) * half + (place[2] ^ k) * piece
            rows = pl.ds(pl.multiple_of(first, piece), piece)
            local = slice(slot * piece, (slot + 1) * piece)
            fresh[:, rows, :] = volume[:, rows, :] - step_size * (left[:, local, :] + right[:, local, :])
            copies.append(pltpu.make_async_copy(fresh.at[:, rows], out.at[:, rows], sems.at[len(copies)]))
            copies[-1].start()
    for copy in copies:
        copy.wait()


def call(kernel, out_shape, in_specs, scratch=(), out_specs=None):
    if out_specs is None:
        out_specs = jax.tree.map(lambda leaf: vmem, out_shape)
    return pl.pallas_call(
        kernel,
        out_shape=out_shape,
        in_specs=in_specs,
        out_specs=out_specs,
        scratch_shapes=list(scratch),
        compiler_params=params,
    )


def in_hbm(value):
    return pltpu.with_memory_space_constraint(value, pltpu.HBM)


def add(left, right):
    return call(add_kernel, jax.ShapeDtypeStruct(left.shape, f32), [vmem] * 2)(left, right)


def shards(volume, projector, tile_ids, counts, ray_counts):
    pix, ang = lax.axis_size("pix"), lax.axis_size("ang")
    own_tiles, slices, width = volume.shape
    ray_blocks = counts.shape[0]
    tile_count, rays, _ = projector.shape
    pixel_tiles = own_tiles * ang
    live = ray_blocks * 5 // 8
    deep = pix // 2
    half, piece = slices // 2, slices // pix
    me, angle = lax.axis_index("pix"), lax.axis_index("ang")
    side, depth = me % 2, me // 2
    place = jnp.stack([side * half + depth * piece, angle, depth, side]).astype(i32)

    across = lambda value, axis, flip: lax.ppermute(
        value, axis, [(d, d ^ flip) for d in range(lax.axis_size(axis))]
    )
    angle_bits = [1 << b for b in range(ang.bit_length() - 1)]

    def after(value, *others):
        return lax.optimization_barrier((value,) + others)[0]

    def spread(value):
        top = angle_bits[-1]
        return {0: value, top: across(value, "ang", top), 1: across(value, "ang", 1)}

    def relay(held, *others):
        top = angle_bits[-1]
        held = dict(held)
        held[top ^ 1] = across(after(held[top], *others), "ang", 1)
        for bit in angle_bits[1:-1]:
            held.update({k ^ bit: across(part, "ang", bit) for k, part in list(held.items())})
        return held

    far = lax.dynamic_slice_in_dim(volume, (1 - side) * half, half, 1)
    near = lax.dynamic_slice_in_dim(volume, side * half, half, 1)
    far_tiles = spread(far)
    near_tiles = spread(near)

    span = tile_count + unroll
    stored = -(-tile_count // group) * group
    listed = jax.ShapeDtypeStruct((2 * span,), i32)
    rank_of, col_of, tile_of, total, picked, split = call(
        functools.partial(front_kernel, own_tiles, ang, live),
        (
            listed,
            listed,
            listed,
            jax.ShapeDtypeStruct((2,), i32),
            jax.ShapeDtypeStruct((live, piece, rays), i32),
            pltpu.VMEM((stored, rays, 2 * width), bf16),
        ),
        [hbm, hbm, smem, hbm, hbm],
        [
            pltpu.SMEM(tile_ids.shape, i32),
            pltpu.SMEM(ray_counts.shape, i32),
            pltpu.SMEM((ray_blocks,), i32),
            pltpu.VMEM((stored, rays, width), f32),
            pltpu.SemaphoreType.DMA((stored // group,)),
            pltpu.SemaphoreType.DMA,
            pltpu.SemaphoreType.DMA((2,)),
        ],
        (smem, smem, smem, smem, vmem, vmem),
    )(in_hbm(tile_ids), in_hbm(ray_counts), place, in_hbm(counts), in_hbm(projector))
    lists = (rank_of, col_of, tile_of)
    rows = jax.ShapeDtypeStruct((live, piece, rays), f32)

    def lists_of(turns):
        return sorted({a // (ang // 2) for a in turns})

    def forward(turns, sides, before=()):
        count = len(sides)
        return call(
            functools.partial(forward_kernel, turns, lists_of(turns), count, span, deep, len(before)),
            (rows,) * deep if before else (pltpu.VMEM((live + 1, half, rays), f32),) * count,
            [smem] * 5 + [vmem] * (1 + count * len(turns) + len(before)),
            [
                pltpu.VMEM((pixel_tiles + 1, 2 * count * half, 2 * width), bf16),
                pltpu.VMEM((live + 1, count * half, rays), f32),
            ],
        )(*lists, total, place, split, *[tiles[a] for tiles in sides for a in turns], *before)

    def backward(turns, part, total, loose=()):
        count = len(part)
        height = piece * count
        made = call(
            functools.partial(backward_kernel, turns, lists_of(turns), loose, count, span),
            sum(
                (
                    (jax.ShapeDtypeStruct((own_tiles, piece, width), f32),) * count
                    if a in loose
                    else (jax.ShapeDtypeStruct((own_tiles, height, width), f32),)
                    for a in turns
                ),
                (),
            ),
            [smem] * 4 + [vmem] * (1 + count),
            [
                pltpu.VMEM((live + 1, 2 * height, rays), bf16),
                pltpu.VMEM((pixel_tiles + 1, height, width), f32),
            ],
        )(*lists, total, split, *[blocks[spot] for spot in part])
        made = list(made)
        return {a: [made.pop(0) for _ in range(count if a in loose else 1)] for a in turns}

    turns = tuple(range(ang))
    early, late = turns[: ang // 2], turns[ang // 2 :]
    if ang > 4:
        far_tiles, near_tiles = relay(far_tiles, total), relay(near_tiles, total)
    far_sums, near_sums = forward(early, (far_tiles, near_tiles))
    if ang <= 4:
        far_tiles, near_tiles = relay(far_tiles, total), relay(near_tiles, near_sums)
    far_parts = forward(late, (far_tiles,), (far_sums,))
    order = list(range(deep - 1, -1, -1))
    crossed = {k: across(far_parts[k], "pix", 1) for k in order}
    near_parts = forward(late, (near_tiles,), (near_sums,))
    side_of = lambda value, k: across(value, "pix", 2 * k)
    came = [side_of(add(near_parts[k], crossed[k]), k) for k in order if k]
    own = call(residual_kernel, rows, [vmem] * (3 + len(came)))(picked, near_parts[0], crossed[0], *came)
    near_blocks = [own] + [side_of(own, k) for k in range(1, deep)]
    blocks = {(0, k): block for k, block in enumerate(near_blocks)}
    arrival = [k for k in (1, 3, 2) if k < deep] + list(range(4, deep))
    for k in [0] + arrival[:-1]:
        blocks[1, k] = across(near_blocks[k], "pix", 1)
    top = angle_bits[-1]
    lower, upper = turns[:top], turns[top:]

    def join(parts):
        return jnp.concatenate(parts, axis=1) if len(parts) > 1 else parts[0]

    def fold(parts, *others):
        parts = dict(parts)
        for bit in angle_bits[:-1]:
            for k in [k for k in parts if k & bit]:
                moved = [across(after(part, *others), "ang", bit) for part in parts.pop(k)]
                parts[k ^ bit] = [join(parts[k ^ bit]) + join(moved)]
        return parts[min(parts)][0]

    def whole(part, total, *others):
        made = backward(turns, part, total, upper[1::2])
        return fold({k: made[k] for k in lower}, *others), fold({k: made[k] for k in upper}, *others)

    def update(parts, terms, *started):
        return pl.pallas_call(
            functools.partial(update_kernel, parts, deep),
            out_shape=jax.ShapeDtypeStruct(volume.shape, f32),
            in_specs=[smem] + [vmem] * (1 + len(terms)) + [anywhere] * len(started),
            out_specs=anywhere,
            scratch_shapes=[pltpu.VMEM(volume.shape, f32), pltpu.SemaphoreType.DMA((2 * deep,))],
            input_output_aliases={2 + len(terms): 0} if started else {},
            compiler_params=params,
        )(place, volume, *terms, *started)

    head = [(0, 0), (0, arrival[0]), (0, arrival[1]), (1, 0)]
    tail = [(1, arrival[-1])]
    middle = [(side, k) for k in arrival for side in range(2) if (side, k) not in head + tail]
    made = backward(turns, head, total, upper[1::2])
    blocks[tail[0]] = across(after(near_blocks[arrival[-1]], made[0][0]), "pix", 1)
    low_head, up_head = fold({k: made[k] for k in lower}), fold({k: made[k] for k in upper})
    came_head = across(up_head, "ang", top)
    made = backward(turns, middle, total)
    ties = [blocks[tail[0]]]
    low_middle, up_middle = fold({k: made[k] for k in lower}, *ties), fold({k: made[k] for k in upper}, *ties)
    came_middle = across(up_middle, "ang", top)
    made = backward(turns, tail, after(total, up_head, up_middle))
    low_tail, up_tail = fold({k: made[k] for k in lower}), fold({k: made[k] for k in upper})
    came_tail = across(up_tail, "ang", top)
    begun = update((head,), (low_head, came_head))
    return update((middle, tail), (low_middle, came_middle, low_tail, came_tail), begun)


def solution(mesh):
    placed = (
        P(("pix", "ang"), None, None),
        P(("pix", "ang"), None, None),
        P(("pix", "ang")),
        P("ang", None, None),
        P("ang", None),
    )
    return jax.shard_map(
        shards, mesh=mesh, in_specs=placed, out_specs=P(("pix", "ang"), None, None), check_vma=False
    )
```

```python
import functools

import jax
import jax.numpy as jnp
from jax import lax
from jax.experimental import pallas as pl
from jax.experimental.pallas import tpu as pltpu
from jax.sharding import PartitionSpec as P

blank_flux = 4096.0
step_size = 0.5
unroll = 20
group = 8
vmem_bytes = 40 * 1024 * 1024

smem = pl.BlockSpec(memory_space=pltpu.SMEM)
vmem = pl.BlockSpec(memory_space=pltpu.VMEM)
hbm = pl.BlockSpec(memory_space=pltpu.HBM)
anywhere = pl.BlockSpec(memory_space=pl.ANY)
params = pltpu.CompilerParams(vmem_limit_bytes=vmem_bytes)
f32, bf16, i32 = jnp.float32, jnp.bfloat16, jnp.int32


def halves(value):
    high = value.astype(bf16)
    return high, (value - high.astype(f32)).astype(bf16)


def front_kernel(own_tiles, angles, live_total, ids_hbm, rays_hbm, place, counts, projector, rank_of, col_of, tile_of, total, picked, split, ids, rays, slot_rank, block, fetched, sem, sides):
    copies = [
        pltpu.make_async_copy(ids_hbm, ids, sides.at[0]),
        pltpu.make_async_copy(rays_hbm, rays, sides.at[1]),
    ]
    for copy in copies:
        copy.start()
    for copy in copies:
        copy.wait()
    tile_count = ids.shape[0]
    span = tile_count + unroll
    pixel_tiles = own_tiles * angles
    ray_blocks = counts.shape[0]
    capacity = ray_blocks // rays.shape[1]
    piece = picked.shape[1]
    width = block.shape[2]
    start = pl.multiple_of(place[0], piece)
    for a in range(2):
        total[a] = 0

    def slot(j, rank):
        live = lax.rem(j, capacity) < rays[0, lax.div(j, capacity)]
        slot_rank[j] = jnp.where(live, rank, -1)

        @pl.when(live)
        def _():
            pltpu.make_async_copy(counts.at[j, pl.ds(start, piece)], picked.at[rank], sem).start()

        return rank + live.astype(i32)

    lax.fori_loop(0, ray_blocks, slot, jnp.int32(0), unroll=4)

    def fetch(t, n):
        pltpu.make_async_copy(projector.at[t], block.at[n], fetched.at[lax.div(n, group)]).start()

    def tile(t, n):
        value = ids[t]
        rank = slot_rank[lax.div(value, pixel_tiles)]

        @pl.when(rank >= 0)
        def _():
            fetch(t, n)
            col = lax.rem(value, pixel_tiles)
            turn = lax.div(col, own_tiles) ^ place[1]
            group_of = lax.div(turn, angles // 2)
            at = total[group_of]
            total[group_of] = at + 1
            at = group_of * span + at
            rank_of[at] = rank
            col_of[at] = turn * own_tiles + lax.rem(col, own_tiles)
            tile_of[at] = n

        return n + (rank >= 0).astype(i32)

    n = lax.fori_loop(0, tile_count, tile, jnp.int32(0), unroll=4)
    groups = lax.div(n + group - 1, group)

    def fill(extra, carry):
        fetch(0, extra)
        return carry

    lax.fori_loop(n, groups * group, fill, 0)
    for a in range(2):
        for extra in range(unroll):
            at = a * span + total[a] + extra
            rank_of[at] = live_total
            col_of[at] = pixel_tiles
            tile_of[at] = 0

    def halve(g, carry):
        rows = pl.ds(g * group, group)
        pltpu.make_async_copy(block.at[rows], block.at[rows], fetched.at[g]).wait()
        for u in range(group):
            high, low = halves(block[g * group + u])
            split[g * group + u, :, :width] = high
            split[g * group + u, :, width:] = low
        return carry

    lax.fori_loop(0, groups, halve, 0)
    pltpu.make_async_copy(picked, picked, sem).wait()


def each(lists, span, total, product, sums, index):
    for a in lists:

        def step(i, carry, a=a):
            base = a * span + i * unroll
            products = [product(base + u) for u in range(unroll)]
            for u in range(unroll):
                sums[index[base + u]] += products[u]
            return carry

        lax.fori_loop(0, lax.div(total[a] + unroll - 1, unroll), step, 0)


def forward_kernel(turns, lists, sides, span, deep, chained, rank_of, col_of, tile_of, total, place, split, *refs):
    tiles, refs = refs[: sides * len(turns)], refs[sides * len(turns) :]
    before, refs = refs[:chained], refs[chained:]
    *outs, packed, sums = refs
    own_tiles, half, width = tiles[0].shape
    piece = half // deep
    rows_all = sides * half

    for at, a in enumerate(turns):

        def fill(i, carry, at=at, a=a):
            for part in range(sides):
                for k in range(deep):
                    rows = pl.ds(pl.multiple_of((place[2] ^ k) * piece, piece), piece)
                    first = part * half + k * piece
                    high, low = halves(tiles[part * len(turns) + at][i, rows, :])
                    for side in range(2):
                        lanes = slice(side * width, (side + 1) * width)
                        packed[a * own_tiles + i, first : first + piece, lanes] = high
                        packed[a * own_tiles + i, rows_all + first : rows_all + first + piece, lanes] = low
            return carry

        lax.fori_loop(0, own_tiles, fill, 0)
    sums[...] = before[0][...] if chained else jnp.zeros_like(sums)

    def product(j):
        both = lax.dot_general(
            packed[col_of[j]], split[tile_of[j]], (((1,), (1,)), ((), ())), preferred_element_type=f32
        )
        return both[:rows_all] + both[rows_all:]

    each(lists, span, total, product, sums, rank_of)
    if not chained:
        for part, out in enumerate(outs):
            out[...] = sums[:, part * half : (part + 1) * half, :]
        return
    for k, out in enumerate(outs):
        out[...] = sums[: out.shape[0], k * piece : (k + 1) * piece, :]


def backward_kernel(turns, lists, loose, count, span, rank_of, col_of, tile_of, total, split, *refs):
    *refs, packed, sums = refs
    blocks, outs = refs[:count], list(refs[count:])
    live, piece, width = blocks[0].shape
    rows_all = piece * count
    own_tiles = outs[0].shape[0]
    zeros = jnp.zeros((own_tiles, rows_all, width), f32)
    for k, block in enumerate(blocks):

        def fill(i, carry, k=k, block=block):
            high, low = halves(block[i])
            packed[i, k * piece : (k + 1) * piece, :] = high
            packed[i, rows_all + k * piece : rows_all + (k + 1) * piece, :] = low
            return carry

        lax.fori_loop(0, live, fill, 0, unroll=4)
    for a in turns:
        sums[a * own_tiles : (a + 1) * own_tiles] = zeros

    def product(j):
        both = jnp.dot(packed[rank_of[j]], split[tile_of[j]], preferred_element_type=f32)
        both = both[:rows_all] + both[rows_all:]
        return both[:, :width] + both[:, width:]

    each(lists, span, total, product, sums, col_of)
    for a in turns:
        tiles = slice(a * own_tiles, (a + 1) * own_tiles)
        if a not in loose:
            outs.pop(0)[...] = sums[tiles]
            continue
        for k in range(count):
            outs.pop(0)[...] = sums[tiles, k * piece : (k + 1) * piece, :]


def add_kernel(left, right, out):
    out[...] = left[...] + right[...]


def residual_kernel(counts, *refs):
    *terms, out = refs
    summed = terms[0][...]
    for term in terms[1:]:
        summed = summed + term[...]
    measured = counts[...].astype(f32)
    out[...] = measured / blank_flux * (summed - jnp.log(blank_flux / measured))


def update_kernel(parts, deep, place, volume, *refs):
    terms, (out, fresh, sems) = refs[: 2 * len(parts)], refs[-3:]
    half = fresh.shape[1] // 2
    piece = half // deep
    copies = []
    for at, part in enumerate(parts):
        left, right = terms[2 * at : 2 * at + 2]
        for slot, (flip, k) in enumerate(part):
            first = (place[3] ^ flip) * half + (place[2] ^ k) * piece
            rows = pl.ds(pl.multiple_of(first, piece), piece)
            local = slice(slot * piece, (slot + 1) * piece)
            fresh[:, rows, :] = volume[:, rows, :] - step_size * (left[:, local, :] + right[:, local, :])
            copies.append(pltpu.make_async_copy(fresh.at[:, rows], out.at[:, rows], sems.at[len(copies)]))
            copies[-1].start()
    for copy in copies:
        copy.wait()


def call(kernel, out_shape, in_specs, scratch=(), out_specs=None):
    if out_specs is None:
        out_specs = jax.tree.map(lambda leaf: vmem, out_shape)
    return pl.pallas_call(
        kernel,
        out_shape=out_shape,
        in_specs=in_specs,
        out_specs=out_specs,
        scratch_shapes=list(scratch),
        compiler_params=params,
    )


def in_hbm(value):
    return pltpu.with_memory_space_constraint(value, pltpu.HBM)


def add(left, right):
    return call(add_kernel, jax.ShapeDtypeStruct(left.shape, f32), [vmem] * 2)(left, right)


def shards(volume, projector, tile_ids, counts, ray_counts):
    pix, ang = lax.axis_size("pix"), lax.axis_size("ang")
    own_tiles, slices, width = volume.shape
    ray_blocks = counts.shape[0]
    tile_count, rays, _ = projector.shape
    pixel_tiles = own_tiles * ang
    live = ray_blocks * 5 // 8
    deep = pix // 2
    half, piece = slices // 2, slices // pix
    me, angle = lax.axis_index("pix"), lax.axis_index("ang")
    side, depth = me % 2, me // 2
    place = jnp.stack([side * half + depth * piece, angle, depth, side]).astype(i32)

    across = lambda value, axis, flip: lax.ppermute(
        value, axis, [(d, d ^ flip) for d in range(lax.axis_size(axis))]
    )
    angle_bits = [1 << b for b in range(ang.bit_length() - 1)]

    def after(value, *others):
        return lax.optimization_barrier((value,) + others)[0]

    def spread(value):
        top = angle_bits[-1]
        return {0: value, top: across(value, "ang", top), 1: across(value, "ang", 1)}

    def relay(held, *others):
        top = angle_bits[-1]
        held = dict(held)
        held[top ^ 1] = across(after(held[top], *others), "ang", 1)
        for bit in angle_bits[1:-1]:
            held.update({k ^ bit: across(part, "ang", bit) for k, part in list(held.items())})
        return held

    far = lax.dynamic_slice_in_dim(volume, (1 - side) * half, half, 1)
    near = lax.dynamic_slice_in_dim(volume, side * half, half, 1)
    far_tiles = spread(far)
    near_tiles = spread(near)

    span = tile_count + unroll
    stored = -(-tile_count // group) * group
    listed = jax.ShapeDtypeStruct((2 * span,), i32)
    rank_of, col_of, tile_of, total, picked, split = call(
        functools.partial(front_kernel, own_tiles, ang, live),
        (
            listed,
            listed,
            listed,
            jax.ShapeDtypeStruct((2,), i32),
            jax.ShapeDtypeStruct((live, piece, rays), i32),
            pltpu.VMEM((stored, rays, 2 * width), bf16),
        ),
        [hbm, hbm, smem, hbm, hbm],
        [
            pltpu.SMEM(tile_ids.shape, i32),
            pltpu.SMEM(ray_counts.shape, i32),
            pltpu.SMEM((ray_blocks,), i32),
            pltpu.VMEM((stored, rays, width), f32),
            pltpu.SemaphoreType.DMA((stored // group,)),
            pltpu.SemaphoreType.DMA,
            pltpu.SemaphoreType.DMA((2,)),
        ],
        (smem, smem, smem, smem, vmem, vmem),
    )(in_hbm(tile_ids), in_hbm(ray_counts), place, in_hbm(counts), in_hbm(projector))
    lists = (rank_of, col_of, tile_of)
    rows = jax.ShapeDtypeStruct((live, piece, rays), f32)

    def lists_of(turns):
        return sorted({a // (ang // 2) for a in turns})

    def forward(turns, sides, before=()):
        count = len(sides)
        return call(
            functools.partial(forward_kernel, turns, lists_of(turns), count, span, deep, len(before)),
            (rows,) * deep if before else (pltpu.VMEM((live + 1, half, rays), f32),) * count,
            [smem] * 5 + [vmem] * (1 + count * len(turns) + len(before)),
            [
                pltpu.VMEM((pixel_tiles + 1, 2 * count * half, 2 * width), bf16),
                pltpu.VMEM((live + 1, count * half, rays), f32),
            ],
        )(*lists, total, place, split, *[tiles[a] for tiles in sides for a in turns], *before)

    def backward(turns, part, total, loose=()):
        count = len(part)
        height = piece * count
        made = call(
            functools.partial(backward_kernel, turns, lists_of(turns), loose, count, span),
            sum(
                (
                    (jax.ShapeDtypeStruct((own_tiles, piece, width), f32),) * count
                    if a in loose
                    else (jax.ShapeDtypeStruct((own_tiles, height, width), f32),)
                    for a in turns
                ),
                (),
            ),
            [smem] * 4 + [vmem] * (1 + count),
            [
                pltpu.VMEM((live + 1, 2 * height, rays), bf16),
                pltpu.VMEM((pixel_tiles + 1, height, width), f32),
            ],
        )(*lists, total, split, *[blocks[spot] for spot in part])
        made = list(made)
        return {a: [made.pop(0) for _ in range(count if a in loose else 1)] for a in turns}

    turns = tuple(range(ang))
    early, late = turns[: ang // 2], turns[ang // 2 :]
    if ang > 4:
        far_tiles, near_tiles = relay(far_tiles, total), relay(near_tiles, total)
    far_sums, near_sums = forward(early, (far_tiles, near_tiles))
    if ang <= 4:
        far_tiles, near_tiles = relay(far_tiles, total), relay(near_tiles, near_sums)
    far_parts = forward(late, (far_tiles,), (far_sums,))
    order = list(range(deep - 1, -1, -1))
    crossed = {k: across(far_parts[k], "pix", 1) for k in order}
    near_parts = forward(late, (near_tiles,), (near_sums,))
    side_of = lambda value, k: across(value, "pix", 2 * k)
    came = [side_of(add(near_parts[k], crossed[k]), k) for k in order if k]
    own = call(residual_kernel, rows, [vmem] * (3 + len(came)))(picked, near_parts[0], crossed[0], *came)
    arrival = [k for k in (1, 2, 3) if k < deep] + list(range(4, deep))
    blocks = {(0, 0): own}
    for k in arrival[:-1]:
        blocks[0, k] = side_of(own, k)
    blocks[0, arrival[-1]] = side_of(after(own, blocks[0, arrival[0]]), arrival[-1])
    near_blocks = [blocks[0, k] for k in range(deep)]
    for k in [0] + arrival[:-1]:
        blocks[1, k] = across(near_blocks[k], "pix", 1)
    top = angle_bits[-1]
    lower, upper = turns[:top], turns[top:]

    def join(parts):
        return jnp.concatenate(parts, axis=1) if len(parts) > 1 else parts[0]

    def fold(parts, *others):
        parts = dict(parts)
        for bit in angle_bits[:-1]:
            for k in [k for k in parts if k & bit]:
                moved = [across(after(part, *others), "ang", bit) for part in parts.pop(k)]
                parts[k ^ bit] = [join(parts[k ^ bit]) + join(moved)]
        return parts[min(parts)][0]

    def whole(part, total, *others):
        made = backward(turns, part, total, upper[1::2])
        return fold({k: made[k] for k in lower}, *others), fold({k: made[k] for k in upper}, *others)

    def update(parts, terms, *started):
        return pl.pallas_call(
            functools.partial(update_kernel, parts, deep),
            out_shape=jax.ShapeDtypeStruct(volume.shape, f32),
            in_specs=[smem] + [vmem] * (1 + len(terms)) + [anywhere] * len(started),
            out_specs=anywhere,
            scratch_shapes=[pltpu.VMEM(volume.shape, f32), pltpu.SemaphoreType.DMA((2 * deep,))],
            input_output_aliases={2 + len(terms): 0} if started else {},
            compiler_params=params,
        )(place, volume, *terms, *started)

    head = [(0, 0), (0, arrival[0]), (0, arrival[1]), (1, 0)]
    tail = [(1, arrival[-1])]
    middle = [(side, k) for k in arrival for side in range(2) if (side, k) not in head + tail]
    made = backward(turns, head, total, upper[1::2])
    blocks[tail[0]] = across(after(near_blocks[arrival[-1]], made[0][0]), "pix", 1)
    low_head, up_head = fold({k: made[k] for k in lower}), fold({k: made[k] for k in upper})
    came_head = across(up_head, "ang", top)
    made = backward(turns, middle, total)
    ties = [blocks[tail[0]]]
    low_middle, up_middle = fold({k: made[k] for k in lower}, *ties), fold({k: made[k] for k in upper}, *ties)
    came_middle = across(up_middle, "ang", top)
    made = backward(turns, tail, after(total, up_head, up_middle))
    low_tail, up_tail = fold({k: made[k] for k in lower}), fold({k: made[k] for k in upper})
    came_tail = across(up_tail, "ang", top)
    begun = update((head,), (low_head, came_head))
    return update((middle, tail), (low_middle, came_middle, low_tail, came_tail), begun)


def solution(mesh):
    placed = (
        P(("pix", "ang"), None, None),
        P(("pix", "ang"), None, None),
        P(("pix", "ang")),
        P("ang", None, None),
        P("ang", None),
    )
    return jax.shard_map(
        shards, mesh=mesh, in_specs=placed, out_specs=P(("pix", "ang"), None, None), check_vma=False
    )
```

```python
import functools

import jax
import jax.numpy as jnp
from jax import lax
from jax.experimental import pallas as pl
from jax.experimental.pallas import tpu as pltpu
from jax.sharding import PartitionSpec as P

blank_flux = 4096.0
step_size = 0.5
unroll = 20
group = 8
vmem_bytes = 40 * 1024 * 1024

smem = pl.BlockSpec(memory_space=pltpu.SMEM)
vmem = pl.BlockSpec(memory_space=pltpu.VMEM)
hbm = pl.BlockSpec(memory_space=pltpu.HBM)
anywhere = pl.BlockSpec(memory_space=pl.ANY)
params = pltpu.CompilerParams(vmem_limit_bytes=vmem_bytes)
f32, bf16, i32 = jnp.float32, jnp.bfloat16, jnp.int32


def halves(value):
    high = value.astype(bf16)
    return high, (value - high.astype(f32)).astype(bf16)


def front_kernel(own_tiles, angles, live_total, ids_hbm, rays_hbm, place, counts, projector, rank_of, col_of, tile_of, total, picked, split, ids, rays, slot_rank, block, fetched, sem, sides):
    copies = [
        pltpu.make_async_copy(ids_hbm, ids, sides.at[0]),
        pltpu.make_async_copy(rays_hbm, rays, sides.at[1]),
    ]
    for copy in copies:
        copy.start()
    for copy in copies:
        copy.wait()
    tile_count = ids.shape[0]
    span = tile_count + unroll
    pixel_tiles = own_tiles * angles
    ray_blocks = counts.shape[0]
    capacity = ray_blocks // rays.shape[1]
    piece = picked.shape[1]
    width = block.shape[2]
    start = pl.multiple_of(place[0], piece)
    for a in range(2):
        total[a] = 0

    def slot(j, rank):
        live = lax.rem(j, capacity) < rays[0, lax.div(j, capacity)]
        slot_rank[j] = jnp.where(live, rank, -1)

        @pl.when(live)
        def _():
            pltpu.make_async_copy(counts.at[j, pl.ds(start, piece)], picked.at[rank], sem).start()

        return rank + live.astype(i32)

    lax.fori_loop(0, ray_blocks, slot, jnp.int32(0), unroll=4)

    def fetch(t, n):
        pltpu.make_async_copy(projector.at[t], block.at[n], fetched.at[lax.div(n, group)]).start()

    def tile(t, n):
        value = ids[t]
        rank = slot_rank[lax.div(value, pixel_tiles)]

        @pl.when(rank >= 0)
        def _():
            fetch(t, n)
            col = lax.rem(value, pixel_tiles)
            turn = lax.div(col, own_tiles) ^ place[1]
            group_of = lax.div(turn, angles // 2)
            at = total[group_of]
            total[group_of] = at + 1
            at = group_of * span + at
            rank_of[at] = rank
            col_of[at] = turn * own_tiles + lax.rem(col, own_tiles)
            tile_of[at] = n

        return n + (rank >= 0).astype(i32)

    n = lax.fori_loop(0, tile_count, tile, jnp.int32(0), unroll=4)
    groups = lax.div(n + group - 1, group)

    def fill(extra, carry):
        fetch(0, extra)
        return carry

    lax.fori_loop(n, groups * group, fill, 0)
    for a in range(2):
        for extra in range(unroll):
            at = a * span + total[a] + extra
            rank_of[at] = live_total
            col_of[at] = pixel_tiles
            tile_of[at] = 0

    def halve(g, carry):
        rows = pl.ds(g * group, group)
        pltpu.make_async_copy(block.at[rows], block.at[rows], fetched.at[g]).wait()
        for u in range(group):
            high, low = halves(block[g * group + u])
            split[g * group + u, :, :width] = high
            split[g * group + u, :, width:] = low
        return carry

    lax.fori_loop(0, groups, halve, 0)
    pltpu.make_async_copy(picked, picked, sem).wait()


def each(lists, span, total, product, sums, index):
    for a in lists:

        def step(i, carry, a=a):
            base = a * span + i * unroll
            products = [product(base + u) for u in range(unroll)]
            for u in range(unroll):
                sums[index[base + u]] += products[u]
            return carry

        lax.fori_loop(0, lax.div(total[a] + unroll - 1, unroll), step, 0)


def forward_kernel(turns, lists, sides, span, deep, chained, rank_of, col_of, tile_of, total, place, split, *refs):
    tiles, refs = refs[: sides * len(turns)], refs[sides * len(turns) :]
    before, refs = refs[:chained], refs[chained:]
    *outs, packed, sums = refs
    own_tiles, half, width = tiles[0].shape
    piece = half // deep
    rows_all = sides * half

    for at, a in enumerate(turns):

        def fill(i, carry, at=at, a=a):
            for part in range(sides):
                for k in range(deep):
                    rows = pl.ds(pl.multiple_of((place[2] ^ k) * piece, piece), piece)
                    first = part * half + k * piece
                    high, low = halves(tiles[part * len(turns) + at][i, rows, :])
                    for side in range(2):
                        lanes = slice(side * width, (side + 1) * width)
                        packed[a * own_tiles + i, first : first + piece, lanes] = high
                        packed[a * own_tiles + i, rows_all + first : rows_all + first + piece, lanes] = low
            return carry

        lax.fori_loop(0, own_tiles, fill, 0)
    sums[...] = before[0][...] if chained else jnp.zeros_like(sums)

    def product(j):
        both = lax.dot_general(
            packed[col_of[j]], split[tile_of[j]], (((1,), (1,)), ((), ())), preferred_element_type=f32
        )
        return both[:rows_all] + both[rows_all:]

    each(lists, span, total, product, sums, rank_of)
    if not chained:
        for part, out in enumerate(outs):
            out[...] = sums[:, part * half : (part + 1) * half, :]
        return
    for k, out in enumerate(outs):
        out[...] = sums[: out.shape[0], k * piece : (k + 1) * piece, :]


def backward_kernel(turns, lists, loose, count, span, rank_of, col_of, tile_of, total, split, *refs):
    *refs, packed, sums = refs
    blocks, outs = refs[:count], list(refs[count:])
    live, piece, width = blocks[0].shape
    rows_all = piece * count
    own_tiles = outs[0].shape[0]
    zeros = jnp.zeros((own_tiles, rows_all, width), f32)
    for k, block in enumerate(blocks):

        def fill(i, carry, k=k, block=block):
            high, low = halves(block[i])
            packed[i, k * piece : (k + 1) * piece, :] = high
            packed[i, rows_all + k * piece : rows_all + (k + 1) * piece, :] = low
            return carry

        lax.fori_loop(0, live, fill, 0, unroll=4)
    for a in turns:
        sums[a * own_tiles : (a + 1) * own_tiles] = zeros

    def product(j):
        both = jnp.dot(packed[rank_of[j]], split[tile_of[j]], preferred_element_type=f32)
        both = both[:rows_all] + both[rows_all:]
        return both[:, :width] + both[:, width:]

    each(lists, span, total, product, sums, col_of)
    for a in turns:
        tiles = slice(a * own_tiles, (a + 1) * own_tiles)
        if a not in loose:
            outs.pop(0)[...] = sums[tiles]
            continue
        for k in range(count):
            outs.pop(0)[...] = sums[tiles, k * piece : (k + 1) * piece, :]


def add_kernel(left, right, out):
    out[...] = left[...] + right[...]


def residual_kernel(counts, *refs):
    *terms, out = refs
    summed = terms[0][...]
    for term in terms[1:]:
        summed = summed + term[...]
    measured = counts[...].astype(f32)
    out[...] = measured / blank_flux * (summed - jnp.log(blank_flux / measured))


def update_kernel(parts, deep, place, volume, *refs):
    terms, (out, fresh, sems) = refs[: 2 * len(parts)], refs[-3:]
    half = fresh.shape[1] // 2
    piece = half // deep
    copies = []
    for at, part in enumerate(parts):
        left, right = terms[2 * at : 2 * at + 2]
        for slot, (flip, k) in enumerate(part):
            first = (place[3] ^ flip) * half + (place[2] ^ k) * piece
            rows = pl.ds(pl.multiple_of(first, piece), piece)
            local = slice(slot * piece, (slot + 1) * piece)
            fresh[:, rows, :] = volume[:, rows, :] - step_size * (left[:, local, :] + right[:, local, :])
            copies.append(pltpu.make_async_copy(fresh.at[:, rows], out.at[:, rows], sems.at[len(copies)]))
            copies[-1].start()
    for copy in copies:
        copy.wait()


def call(kernel, out_shape, in_specs, scratch=(), out_specs=None):
    if out_specs is None:
        out_specs = jax.tree.map(lambda leaf: vmem, out_shape)
    return pl.pallas_call(
        kernel,
        out_shape=out_shape,
        in_specs=in_specs,
        out_specs=out_specs,
        scratch_shapes=list(scratch),
        compiler_params=params,
    )


def in_hbm(value):
    return pltpu.with_memory_space_constraint(value, pltpu.HBM)


def add(left, right):
    return call(add_kernel, jax.ShapeDtypeStruct(left.shape, f32), [vmem] * 2)(left, right)


def shards(volume, projector, tile_ids, counts, ray_counts):
    pix, ang = lax.axis_size("pix"), lax.axis_size("ang")
    own_tiles, slices, width = volume.shape
    ray_blocks = counts.shape[0]
    tile_count, rays, _ = projector.shape
    pixel_tiles = own_tiles * ang
    live = ray_blocks * 5 // 8
    deep = pix // 2
    half, piece = slices // 2, slices // pix
    me, angle = lax.axis_index("pix"), lax.axis_index("ang")
    side, depth = me % 2, me // 2
    place = jnp.stack([side * half + depth * piece, angle, depth, side]).astype(i32)

    across = lambda value, axis, flip: lax.ppermute(
        value, axis, [(d, d ^ flip) for d in range(lax.axis_size(axis))]
    )
    angle_bits = [1 << b for b in range(ang.bit_length() - 1)]

    def after(value, *others):
        return lax.optimization_barrier((value,) + others)[0]

    def spread(value):
        top = angle_bits[-1]
        return {0: value, top: across(value, "ang", top), 1: across(value, "ang", 1)}

    def relay(held, *others):
        top = angle_bits[-1]
        held = dict(held)
        held[top ^ 1] = across(after(held[top], *others), "ang", 1)
        for bit in angle_bits[1:-1]:
            held.update({k ^ bit: across(part, "ang", bit) for k, part in list(held.items())})
        return held

    far = lax.dynamic_slice_in_dim(volume, (1 - side) * half, half, 1)
    near = lax.dynamic_slice_in_dim(volume, side * half, half, 1)
    far_tiles = spread(far)
    near_tiles = spread(near)

    span = tile_count + unroll
    stored = -(-tile_count // group) * group
    listed = jax.ShapeDtypeStruct((2 * span,), i32)
    rank_of, col_of, tile_of, total, picked, split = call(
        functools.partial(front_kernel, own_tiles, ang, live),
        (
            listed,
            listed,
            listed,
            jax.ShapeDtypeStruct((2,), i32),
            jax.ShapeDtypeStruct((live, piece, rays), i32),
            pltpu.VMEM((stored, rays, 2 * width), bf16),
        ),
        [hbm, hbm, smem, hbm, hbm],
        [
            pltpu.SMEM(tile_ids.shape, i32),
            pltpu.SMEM(ray_counts.shape, i32),
            pltpu.SMEM((ray_blocks,), i32),
            pltpu.VMEM((stored, rays, width), f32),
            pltpu.SemaphoreType.DMA((stored // group,)),
            pltpu.SemaphoreType.DMA,
            pltpu.SemaphoreType.DMA((2,)),
        ],
        (smem, smem, smem, smem, vmem, vmem),
    )(in_hbm(tile_ids), in_hbm(ray_counts), place, in_hbm(counts), in_hbm(projector))
    lists = (rank_of, col_of, tile_of)
    rows = jax.ShapeDtypeStruct((live, piece, rays), f32)

    def lists_of(turns):
        return sorted({a // (ang // 2) for a in turns})

    def forward(turns, sides, before=()):
        count = len(sides)
        return call(
            functools.partial(forward_kernel, turns, lists_of(turns), count, span, deep, len(before)),
            (rows,) * deep if before else (pltpu.VMEM((live + 1, half, rays), f32),) * count,
            [smem] * 5 + [vmem] * (1 + count * len(turns) + len(before)),
            [
                pltpu.VMEM((pixel_tiles + 1, 2 * count * half, 2 * width), bf16),
                pltpu.VMEM((live + 1, count * half, rays), f32),
            ],
        )(*lists, total, place, split, *[tiles[a] for tiles in sides for a in turns], *before)

    def backward(turns, part, total, loose=()):
        count = len(part)
        height = piece * count
        made = call(
            functools.partial(backward_kernel, turns, lists_of(turns), loose, count, span),
            sum(
                (
                    (jax.ShapeDtypeStruct((own_tiles, piece, width), f32),) * count
                    if a in loose
                    else (jax.ShapeDtypeStruct((own_tiles, height, width), f32),)
                    for a in turns
                ),
                (),
            ),
            [smem] * 4 + [vmem] * (1 + count),
            [
                pltpu.VMEM((live + 1, 2 * height, rays), bf16),
                pltpu.VMEM((pixel_tiles + 1, height, width), f32),
            ],
        )(*lists, total, split, *[blocks[spot] for spot in part])
        made = list(made)
        return {a: [made.pop(0) for _ in range(count if a in loose else 1)] for a in turns}

    turns = tuple(range(ang))
    early, late = turns[: ang // 2], turns[ang // 2 :]
    if ang > 4:
        far_tiles, near_tiles = relay(far_tiles, total), relay(near_tiles, total)
    far_sums, near_sums = forward(early, (far_tiles, near_tiles))
    if ang <= 4:
        far_tiles, near_tiles = relay(far_tiles, total), relay(near_tiles, near_sums)
    far_parts = forward(late, (far_tiles,), (far_sums,))
    order = list(range(deep - 1, -1, -1))
    crossed = {k: across(far_parts[k], "pix", 1) for k in order}
    near_parts = forward(late, (near_tiles,), (near_sums,))
    side_of = lambda value, k: across(value, "pix", 2 * k)
    came = [side_of(add(near_parts[k], crossed[k]), k) for k in order if k]
    own = call(residual_kernel, rows, [vmem] * (3 + len(came)))(picked, near_parts[0], crossed[0], *came)
    arrival = [k for k in (1, 2, 3) if k < deep] + list(range(4, deep))
    blocks = {(0, 0): own}
    for k in arrival[:-1]:
        blocks[0, k] = side_of(own, k)
    blocks[0, arrival[-1]] = side_of(after(own, blocks[0, arrival[0]]), arrival[-1])
    near_blocks = [blocks[0, k] for k in range(deep)]
    for k in [0] + arrival[:-1]:
        blocks[1, k] = across(near_blocks[k], "pix", 1)
    top = angle_bits[-1]
    lower, upper = turns[:top], turns[top:]

    def join(parts):
        return jnp.concatenate(parts, axis=1) if len(parts) > 1 else parts[0]

    def fold(parts, *others):
        parts = dict(parts)
        for bit in angle_bits[:-1]:
            for k in [k for k in parts if k & bit]:
                moved = [across(after(part, *others), "ang", bit) for part in parts.pop(k)]
                parts[k ^ bit] = [join(parts[k ^ bit]) + join(moved)]
        return parts[min(parts)][0]

    def whole(part, total, *others):
        made = backward(turns, part, total, upper[1::2])
        return fold({k: made[k] for k in lower}, *others), fold({k: made[k] for k in upper}, *others)

    def update(parts, terms, *started):
        return pl.pallas_call(
            functools.partial(update_kernel, parts, deep),
            out_shape=jax.ShapeDtypeStruct(volume.shape, f32),
            in_specs=[smem] + [vmem] * (1 + len(terms)) + [anywhere] * len(started),
            out_specs=anywhere,
            scratch_shapes=[pltpu.VMEM(volume.shape, f32), pltpu.SemaphoreType.DMA((2 * deep,))],
            input_output_aliases={2 + len(terms): 0} if started else {},
            compiler_params=params,
        )(place, volume, *terms, *started)

    head = [(0, 0), (0, arrival[0]), (0, arrival[1]), (1, 0)]
    tail = [(1, arrival[-1])]
    middle = [(side, k) for k in arrival for side in range(2) if (side, k) not in head + tail]
    made = backward(turns, head, total, upper[1::2])
    blocks[tail[0]] = across(after(near_blocks[arrival[-1]], made[0][0]), "pix", 1)
    ties = [blocks[1, k] for k in arrival[:-1]]
    low_head, up_head = fold({k: made[k] for k in lower}), fold({k: made[k] for k in upper}, *ties)
    came_head = across(up_head, "ang", top)
    made = backward(turns, middle, total)
    ties = [blocks[tail[0]]]
    low_middle, up_middle = fold({k: made[k] for k in lower}, *ties), fold({k: made[k] for k in upper}, *ties)
    came_middle = across(up_middle, "ang", top)
    made = backward(turns, tail, after(total, came_head, up_middle))
    low_tail, up_tail = fold({k: made[k] for k in lower}), fold({k: made[k] for k in upper})
    came_tail = across(up_tail, "ang", top)
    begun = update((head,), (low_head, came_head))
    return update((middle, tail), (low_middle, came_middle, low_tail, came_tail), begun)


def solution(mesh):
    placed = (
        P(("pix", "ang"), None, None),
        P(("pix", "ang"), None, None),
        P(("pix", "ang")),
        P("ang", None, None),
        P("ang", None),
    )
    return jax.shard_map(
        shards, mesh=mesh, in_specs=placed, out_specs=P(("pix", "ang"), None, None), check_vma=False
    )
```
